256 devices in a mesh: dp: 64 (over z, y, core), grp: 4 (over x).
Axes of the slice: x: 4, y: 4, z: 8, core: 2. Of those that a mesh axis runs over, the one named last changes fastest.
Arguments:
- grads: bfloat16 [64, 8, 2048, 128], P('dp', 'grp'), parts along dimension 1, may hold values from -6 to 6
- residual: float32 [64, 8, 2048, 128], P('dp', 'grp'), parts along dimension 1, may hold values from -4 to 4
- params: float32 [8, 2048, 128], P('grp'), parts along dimension 0, may hold values from -6 to 6
- momentum: float32 [8, 64, 63, 128], P('grp', 'dp'), parts along dimension 0, may hold values from -6 to 6
- indices: int32 [64, 8, 16], P('dp', 'grp'), parts along dimension 1, may hold values from 0 to 2047, as said below
- counts: int32 [64, 8], P('dp', 'grp'), parts along dimension 1, may hold values from 1 to 16
- region_sizes: int32 [8, 64], P('grp'), parts along dimension 0, may hold values from 1 to 63, as said below
Outputs:
- new_residual: float32 [64, 8, 2048, 128], P('dp', 'grp'), parts along dimension 1
- new_momentum: float32 [8, 64, 63, 128], P('grp', 'dp'), parts along dimension 0
- new_params: float32 [8, 2048, 128], P('grp'), parts along dimension 0
The draws below stay inside these ranges and needn't reach their ends.
There are 4 independent parts, one for each index of `grp`. The reference program is written for one: setup_inputs(seed, part) draws one part's arguments, and reference() takes and returns one part's arrays. A program takes and returns all parts, laid end to end along the dimension named above; each array names one. Nothing has to cross between parts.
Inputs may be any that keep to these rules, and one draw needn't show every extreme that they name: `indices`: the 16 entries of one replica's list for one bucket are distinct. `region_sizes`: a bucket's sizes sum to 2048.
All inputs are finite; a program needn't handle non-finite values.
Results may differ from the reference program's by a relative error of at most 0.0003.
Values sent between devices are 32-bit elements; how exact they have to be, the bound alone decides.
A program may use at most 64 MiB of HBM per device.

```python
import jax
import jax.numpy as jnp

NB = 2048
K = 16
BLK = 128
RMAX = 63
N_DP = 64


def draw_indices(key, part):
    key = jax.random.fold_in(key, 11)
    group_key, score_key = jax.random.split(key)
    hot_groups = jax.random.randint(group_key, (2, 32), 0, 4) == 0
    group_of = jnp.arange(NB, dtype=jnp.int32) * 32 // NB
    block_hot = hot_groups[:, group_of].astype(jnp.int32)
    noise = jax.random.randint(score_key, (N_DP, 2, NB), 0, 1 << 18)
    scores = (noise + block_hot[None, :, :] * (1 << 18)) * NB + jnp.arange(NB, dtype=jnp.int32)[None, None, :]
    picked = jax.lax.top_k(scores, K)[1]
    return picked.astype(jnp.int32)


def draw_counts(key, part):
    key = jax.random.fold_in(key, 12)
    first_key, second_key = jax.random.split(key)
    drawn = jax.random.randint(first_key, (N_DP, 2), 1, K + 1)
    forced = jax.random.randint(second_key, (2,), 0, N_DP)
    device_ids = jnp.arange(N_DP, dtype=jnp.int32)[:, None]
    return jnp.where(device_ids == forced[None, :], K, drawn).astype(jnp.int32)


def draw_region_sizes(key, part):
    key = jax.random.fold_in(key, 13)
    perm_key, shift_key = jax.random.split(key)
    middle = NB // N_DP
    half = N_DP // 2
    orders = jax.vmap(lambda sub: jax.random.permutation(sub, N_DP))(jax.random.split(perm_key, 2))
    shifts = jax.random.randint(shift_key, (2, half), 0, middle)
    shifts = shifts.at[:, 0].set(middle - 1)
    bucket_ids = jnp.arange(2, dtype=jnp.int32)[:, None]
    extents = jnp.zeros((2, N_DP), jnp.int32)
    extents = extents.at[bucket_ids, orders[:, :half]].set(middle + shifts)
    extents = extents.at[bucket_ids, orders[:, half:]].set(middle - shifts)
    return extents.astype(jnp.int32)


def shard_levels(key, dims, cuts, low, high):
    gain = 1.0
    for axis_at, shards_of in cuts:
        draws = jax.random.uniform(jax.random.fold_in(jax.random.fold_in(key, 6), axis_at), (shards_of,), jnp.float32, low / len(cuts), high / len(cuts))
        gain = gain * jnp.repeat(jnp.exp(draws), dims[axis_at] // shards_of).reshape((-1,) + (1,) * (len(dims) - 1 - axis_at))
    return gain


def centred(stream_key, extent, width, reach, cuts=(), held_as=jnp.bfloat16):
    entries = jax.random.normal(stream_key, extent, jnp.float32) * width
    if len(cuts) > 0:
        entries = shard_levels(stream_key, extent, cuts, -0.22, 0.18) * entries
    return jnp.clip(entries, min=-reach, max=reach).astype(held_as)


def setup_inputs(seed: int = 0, part: int = 0) -> dict:
    streams_of = jax.random.split(jax.random.key(seed), 8)
    part_splits = jax.random.split(jax.random.fold_in(streams_of[7], part), 8)
    grads = centred(part_splits[0], (N_DP, 2, NB, BLK), 1.0, 6.0, ((0, 64),))
    residual = centred(part_splits[1], (N_DP, 2, NB, BLK), 0.5, 4.0, ((0, 64),), jnp.float32)
    params = centred(part_splits[2], (2, NB, BLK), 1.0, 6.0, (), jnp.float32)
    momentum = centred(part_splits[3], (2, N_DP, RMAX, BLK), 1.0, 6.0, ((1, 64),), jnp.float32)
    indices = draw_indices(jax.random.fold_in(jax.random.fold_in(streams_of[7], part), 71), part)
    counts = draw_counts(jax.random.fold_in(jax.random.fold_in(streams_of[7], part), 71), part)
    region_sizes = draw_region_sizes(jax.random.fold_in(jax.random.fold_in(streams_of[7], part), 71), part)
    return {"grads": grads, "residual": residual, "params": params, "momentum": momentum, "indices": indices, "counts": counts, "region_sizes": region_sizes}


decay_rate = 0.9
learn_rate = 0.1


def reference(grads, residual, params, momentum, indices, counts, region_sizes):
    residual_list = []
    momentum_list = []
    params_list = []
    blocks = jnp.arange(NB, dtype=jnp.int32)
    slot_ids = jnp.arange(RMAX, dtype=jnp.int32)
    for bucket in range(2):
        accumulated = residual[:, bucket] + grads[:, bucket].astype(jnp.float32)
        active = jnp.arange(K, dtype=jnp.int32)[None, :] < counts[:, bucket][:, None]
        matches = (indices[:, bucket][:, :, None] == blocks[None, None, :]) & active[:, :, None]
        chosen = jnp.any(matches, axis=1)
        total = jnp.sum(jnp.where(chosen[:, :, None], accumulated, jnp.float32(0.0)), axis=0)
        residual_list.append(jnp.where(chosen[:, :, None], jnp.float32(0.0), accumulated))
        extents = region_sizes[bucket].astype(jnp.int32)
        starts = (jnp.cumsum(extents) - extents).astype(jnp.int32)
        row_ids = jnp.clip(starts[:, None] + slot_ids[None, :], 0, NB - 1).astype(jnp.int32)
        in_region = slot_ids[None, :] < extents[:, None]
        fresh = jnp.where(in_region[:, :, None], decay_rate * momentum[bucket] + total[row_ids], jnp.float32(0.0))
        momentum_list.append(fresh)
        owners = jnp.sum((starts[None, 1:] <= blocks[:, None]).astype(jnp.int32), axis=1).astype(jnp.int32)
        offset = (blocks - starts[owners]).astype(jnp.int32)
        params_list.append(params[bucket] - learn_rate * fresh[owners, offset])
    return (jnp.stack(residual_list, axis=1), jnp.stack(momentum_list), jnp.stack(params_list))
```

```python
import functools
import heapq

import jax
import jax.numpy as jnp
from jax import lax
from jax.experimental import pallas as pl
from jax.experimental.pallas import tpu as pltpu
from jax.sharding import PartitionSpec as P

decay_rate = 0.9
learn_rate = 0.1

NZ, NY = 8, 4
SLOTS = NZ * NY
ROWS = 160
MESH = pl.DeviceIdType.MESH
CHUNKS = 4


def z_first(rows):
    children = {}
    for ry in range(NY):
        for rz in range(NZ):
            children[(rz, ry)] = []
    for a, b in ((0, 1), (1, 2), (2, 3), (3, 4), (0, 7), (7, 6), (6, 5)):
        children[(a, 0)].append((b, 0))
    for rz in range(NZ):
        for a, b in ((0, 1), (1, 2), (0, 3)):
            children[(rz, a)].append((rz, b))
    return rows, children


def y_first(rows):
    children = {}
    for ry in range(NY):
        for rz in range(NZ):
            children[(rz, ry)] = []
    for a, b in ((0, 1), (1, 2), (0, 3)):
        children[(0, a)].append((0, b))
    for ry in range(NY):
        for a, b in ((0, 1), (1, 2), (2, 3), (3, 4), (0, 7), (7, 6), (6, 5)):
            children[(a, ry)].append((b, ry))
    return rows, children


FLOWS = (z_first((0, 96)), y_first((96, 160)))


def schedule(flows):
    def height(children, node):
        return 1 + max((height(children, c) for c in children[node]), default=0)

    heap = [(0.0, f, (0, 0)) for f in range(len(flows))]
    free = {"z": 0.0, "y": 0.0}
    now, order = 0.0, []
    while heap:
        at, f, node = heapq.heappop(heap)
        now = max(now, at) + 0.05
        (first, last), children = flows[f]
        kids = sorted(children[node], key=lambda c: -height(children, c))
        order.append((f, node, kids))
        for kid in kids:
            now += 0.07
            axis = "z" if kid[1] == node[1] else "y"
            free[axis] = max(free[axis], now) + (last - first) * 512 / 105e3
            heapq.heappush(heap, (free[axis] + 1.9, f, kid))
    return order


ORDER = schedule(FLOWS)


def slot_of(node):
    return node[0] * NY + node[1]


def gather_kernel(
    idx_s, cnt_s, idx_v, grads, residual, momentum,
    everyone, acc_out,
    gbuf, rbuf, abuf, send_sem, recv_sem, pair_send, pair_recv, in_sem, mom_sem, out_sem,
):
    me = lax.axis_index("dp")
    core = lax.rem(me, 2)
    y = lax.rem(lax.div(me, 2), NY)
    z = lax.div(me, 2 * NY)
    turn = 1 - 2 * core

    def at(dz, dy):
        return (lax.rem(z + turn * dz + NZ, NZ) * NY + lax.rem(y + turn * dy + NY, NY)) * 2 + core

    sibling = me + turn
    targets = {(1, 0): at(1, 0), (7, 0): at(-1, 0), (0, 1): at(0, 1), (0, 3): at(0, -1)}

    barrier = pltpu.get_barrier_semaphore()
    for t in list(targets.values()) + [sibling]:
        pl.semaphore_signal(barrier, inc=1, device_id={"dp": t}, device_id_type=MESH)

    nb = residual.shape[2]
    part = nb // CHUNKS
    for b in range(2):
        pltpu.make_async_copy(
            momentum.at[b, 0], everyone.at[0, 0, pl.ds(64 * b, 63)], mom_sem.at[b]
        ).start()
    loads = []
    for b in range(2):
        for k in range(CHUNKS):
            span = pl.ds(k * part, part)
            j = b * CHUNKS + k
            g = pltpu.make_async_copy(grads.at[0, b, span], gbuf.at[b, span], in_sem.at[0, j])
            r = pltpu.make_async_copy(residual.at[0, b, span], rbuf.at[b, span], in_sem.at[1, j])
            g.start()
            r.start()
            loads.append((g, r))
    for b in range(2):
        everyone[0, 0, pl.ds(64 * b + 63, 1), :] = jnp.zeros((1, 128), jnp.float32)
        everyone[0, 0, pl.ds(64 * b + 63, 1), 0:16] = idx_v[0, pl.ds(b, 1), :].astype(jnp.float32)
    stores = []
    for b in range(2):
        for k in range(CHUNKS):
            j = b * CHUNKS + k
            span = pl.ds(k * part, part)
            g, r = loads[j]
            g.wait()
            r.wait()
            abuf[b, span, :] = rbuf[b, span, :] + gbuf[b, span, :].astype(jnp.float32)
            s = pltpu.make_async_copy(abuf.at[b, span], acc_out.at[b, span], out_sem.at[j])
            s.start()
            stores.append(s)
    for b in range(2):
        for i in range(16):
            row = abuf[b, pl.ds(idx_s[0, b, i], 1), :]
            everyone[0, 0, pl.ds(128 + 16 * b + i, 1), :] = jnp.where(
                i < cnt_s[0, b], row, jnp.float32(0.0)
            )
    for b in range(2):
        pltpu.make_async_copy(
            momentum.at[b, 0], everyone.at[0, 0, pl.ds(64 * b, 63)], mom_sem.at[b]
        ).wait()
    pl.semaphore_wait(barrier, 5)

    def piece(f, node, side=0):
        first, last = FLOWS[f][0]
        return everyone.at[side, slot_of(node), pl.ds(first, last - first)]

    def hop(f, node, kid):
        step = ((kid[0] - node[0]) % NZ, (kid[1] - node[1]) % NY)
        return pltpu.make_async_remote_copy(
            src_ref=piece(f, node),
            dst_ref=piece(f, kid),
            send_sem=send_sem.at[f, slot_of(kid)],
            recv_sem=recv_sem.at[f, slot_of(kid)],
            device_id={"dp": targets[step]},
            device_id_type=MESH,
        )

    def across(f, node):
        return pltpu.make_async_remote_copy(
            src_ref=piece(f, node),
            dst_ref=piece(f, node, 1),
            send_sem=pair_send.at[f, slot_of(node)],
            recv_sem=pair_recv.at[f, slot_of(node)],
            device_id={"dp": sibling},
            device_id_type=MESH,
        )

    parent = {(f, kid): node for f, node, kids in ORDER for kid in kids}
    for f, node, kids in ORDER:
        if node != (0, 0):
            hop(f, parent[(f, node)], node).wait_recv()
        for kid in kids:
            hop(f, node, kid).start()
        across(f, node).start()
    for f, node, kids in ORDER:
        across(f, node).wait_recv()
    for f, node, kids in ORDER:
        for kid in kids:
            hop(f, node, kid).wait_send()
        across(f, node).wait_send()
    for s in stores:
        s.wait()


def update_kernel(
    sizes, idx_own, cnt, everyone, acc, params,
    new_residual, new_momentum, new_params,
    pbuf, nm, lists_v, lists_s, zero_row, res_sem, row_sem, in_sem, out_sem, list_sem,
):
    me = lax.axis_index("dp")
    core = lax.rem(me, 2)
    y = lax.rem(lax.div(me, 2), NY)
    z = lax.div(me, 2 * NY)
    nb = params.shape[1]
    move = pltpu.make_async_copy(acc, new_residual.at[0], res_sem)
    move.start()
    load = pltpu.make_async_copy(params, pbuf, in_sem)
    load.start()
    zero_row[...] = jnp.zeros_like(zero_row)

    def place_of(o):
        oz, oy, oc = lax.shift_right_logical(o, 3), lax.shift_right_logical(o, 1) & 3, o & 1
        turn = 1 - 2 * oc
        slot = ((turn * (z - oz)) & (NZ - 1)) * NY + ((turn * (y - oy)) & (NY - 1))
        return (oc + core) & 1, slot

    def read_list(o, carry):
        side, slot = place_of(o)
        for b in range(2):
            lists_v[b, pl.ds(o, 1), :] = everyone[side, slot, pl.ds(64 * b + 63, 1), :].astype(jnp.int32)
        return carry

    lax.fori_loop(0, 64, read_list, 0, unroll=8)
    fetch = pltpu.make_async_copy(lists_v, lists_s, list_sem)
    fetch.start()

    def place(o, carry):
        s0, s1, m0, m1 = carry
        side, slot = place_of(o)
        nm[0, pl.ds(s0, 64), :] = decay_rate * everyone[side, slot, 0:64, :]
        nm[1, pl.ds(s1, 64), :] = decay_rate * everyone[side, slot, 64:128, :]
        m0 = jnp.where(o == me, s0, m0)
        m1 = jnp.where(o == me, s1, m1)
        return s0 + sizes[0, o], s1 + sizes[1, o], m0, m1

    zero = jnp.int32(0)
    _, _, m0, m1 = lax.fori_loop(0, 64, place, (zero, zero, zero, zero), unroll=4)
    fetch.wait()

    def add(o, carry):
        side, slot = place_of(o)
        rows = []
        for b in range(2):
            for i in range(16):
                j = lists_s[b, o, i]
                rows.append((b, j, nm[b, pl.ds(j, 1), :] + everyone[side, slot, pl.ds(128 + 16 * b + i, 1), :]))
        for b, j, row in rows:
            nm[b, pl.ds(j, 1), :] = row
        return carry

    lax.fori_loop(0, 64, add, 0, unroll=2)
    load.wait()
    part = nb // CHUNKS
    outs = []
    for b in range(2):
        for k in range(CHUNKS):
            span = pl.ds(k * part, part)
            pbuf[b, span, :] = pbuf[b, span, :] - learn_rate * nm[b, span, :]
            out = pltpu.make_async_copy(pbuf.at[b, span], new_params.at[b, span], out_sem.at[b * CHUNKS + k])
            out.start()
            outs.append(out)
    rows = new_momentum.shape[2]
    for b, first in ((0, m0), (1, m1)):
        mine = nm[b, pl.ds(first, rows), :]
        inside = lax.broadcasted_iota(jnp.int32, (rows, 128), 0) < sizes[b, me]
        new_momentum[b, 0] = jnp.where(inside, mine, jnp.float32(0.0))
    move.wait()

    def clear(b, i):
        return pltpu.make_async_copy(
            zero_row, new_residual.at[0, b, pl.ds(idx_own[0, b, i], 1)], row_sem.at[b, i]
        )

    for b in range(2):
        for i in range(16):

            @pl.when(i < cnt[0, b])
            def _():
                clear(b, i).start()

    for b in range(2):
        for i in range(16):

            @pl.when(i < cnt[0, b])
            def _():
                clear(b, i).wait()

    for out in outs:
        out.wait()


def on_device(grads, residual, params, momentum, indices, counts, region_sizes):
    nb = grads.shape[2]
    any_space = pl.BlockSpec(memory_space=pl.ANY)
    vmem = pl.BlockSpec(memory_space=pltpu.VMEM)
    smem = pl.BlockSpec(memory_space=pltpu.SMEM)
    dma = pltpu.SemaphoreType.DMA
    everyone, acc = pl.pallas_call(
        gather_kernel,
        out_shape=(
            jax.ShapeDtypeStruct((2, SLOTS, ROWS, 128), jnp.float32),
            jax.ShapeDtypeStruct((2, nb, 128), jnp.float32),
        ),
        in_specs=[smem, smem, vmem, any_space, any_space, any_space],
        out_specs=(vmem, any_space),
        scratch_shapes=[
            pltpu.VMEM((2, nb, 128), jnp.bfloat16),
            pltpu.VMEM((2, nb, 128), jnp.float32),
            pltpu.VMEM((2, nb, 128), jnp.float32),
            dma((len(FLOWS), SLOTS)),
            dma((len(FLOWS), SLOTS)),
            dma((len(FLOWS), SLOTS)),
            dma((len(FLOWS), SLOTS)),
            dma((2, 2 * CHUNKS)),
            dma((2,)),
            dma((2 * CHUNKS,)),
        ],
        compiler_params=pltpu.CompilerParams(
            collective_id=0, has_side_effects=True, vmem_limit_bytes=32 << 20
        ),
        name="gather",
    )(indices, counts, indices, grads, residual, momentum)
    return pl.pallas_call(
        update_kernel,
        out_shape=(
            jax.ShapeDtypeStruct((1, 2, nb, 128), jnp.float32),
            jax.ShapeDtypeStruct(momentum.shape, jnp.float32),
            jax.ShapeDtypeStruct(params.shape, jnp.float32),
        ),
        in_specs=[smem, smem, smem, vmem, any_space, any_space],
        out_specs=(any_space, vmem, any_space),
        scratch_shapes=[
            pltpu.VMEM((2, nb, 128), jnp.float32),
            pltpu.VMEM((2, nb + 64, 128), jnp.float32),
            pltpu.VMEM((2, 64, 128), jnp.int32),
            pltpu.SMEM((2, 64, 128), jnp.int32),
            pltpu.VMEM((1, 128), jnp.float32),
            dma,
            dma((2, 16)),
            dma,
            dma((2 * CHUNKS,)),
            dma,
        ],
        compiler_params=pltpu.CompilerParams(vmem_limit_bytes=32 << 20),
        name="update",
    )(region_sizes, indices, counts, everyone, acc, params)


def solution(mesh):
    placed = (
        P("dp", "grp", None, None),
        P("dp", "grp", None, None),
        P("grp", None, None),
        P("grp", "dp", None, None),
        P("dp", "grp", None),
        P("dp", "grp"),
        P("grp", None),
    )
    return jax.shard_map(
        on_device,
        mesh=mesh,
        in_specs=placed,
        out_specs=(P("dp", "grp", None, None), P("grp", "dp", None, None), P("grp", None, None)),
        check_vma=False,
    )
```

```python
import functools
import heapq

import jax
import jax.numpy as jnp
from jax import lax
from jax.experimental import pallas as pl
from jax.experimental.pallas import tpu as pltpu
from jax.sharding import PartitionSpec as P

decay_rate = 0.9
learn_rate = 0.1

NZ, NY = 8, 4
SLOTS = NZ * NY
ROWS = 160
MESH = pl.DeviceIdType.MESH
CHUNKS = 4
PITCH = 2048 + 64


Z_TREES = {
    4: ((0, 1), (1, 2), (2, 3), (3, 4), (0, 7), (7, 6), (6, 5)),
    3: ((0, 1), (1, 2), (2, 3), (2, 4), (0, 7), (7, 6), (6, 5)),
    2: ((0, 1), (0, 2), (2, 3), (2, 4), (0, 7), (0, 6), (6, 5)),
    1: ((0, 1), (0, 2), (0, 3), (0, 4), (0, 7), (0, 6), (0, 5)),
}
Y_TREES = {2: ((0, 1), (1, 2), (0, 3)), 1: ((0, 1), (0, 2), (0, 3))}

FLOWS = (
    (0, 96, True, 3, 1, False),
    (96, 160, False, 3, 1, True),
)


def tree_of(flow):
    _, _, along_z, zt, yt, _ = flow
    children = {(rz, ry): [] for rz in range(NZ) for ry in range(NY)}
    for a, b in Z_TREES[zt]:
        for ry in range(1 if along_z else NY):
            children[(a, ry)].append((b, ry))
    for a, b in Y_TREES[yt]:
        for rz in range(NZ if along_z else 1):
            children[(rz, a)].append((rz, b))
    return children


TREES = tuple(tree_of(flow) for flow in FLOWS)


def step_of(node, kid):
    dz, dy = (kid[0] - node[0]) % NZ, (kid[1] - node[1]) % NY
    return (dz if 2 * dz <= NZ else dz - NZ), (dy if 2 * dy <= NY else dy - NY)


STEPS = tuple(sorted({step_of(n, k) for t in TREES for n, kids in t.items() for k in kids}))
LATENCY, PER_HOP, PICKS = 1.6, 0.65, 1.5


def schedule():
    def height(f, node):
        return 1 + max((height(f, c) for c in TREES[f][node]), default=0)

    heap = [(PICKS if FLOWS[f][5] else 0.0, f, (0, 0)) for f in range(len(FLOWS))]
    free = {"z": 0.0, "y": 0.0}
    now, order = 0.0, []
    while heap:
        at, f, node = heapq.heappop(heap)
        now = max(now, at) + 0.05
        kids = sorted(TREES[f][node], key=lambda c: -height(f, c))
        order.append((f, node, kids))
        for kid in kids:
            now += 0.07
            dz, dy = step_of(node, kid)
            axis, hops = ("z", abs(dz)) if dz else ("y", abs(dy))
            free[axis] = max(free[axis], now) + hops * (FLOWS[f][1] - FLOWS[f][0]) * 512 / 105e3
            heapq.heappush(heap, (free[axis] + LATENCY + hops * PER_HOP, f, kid))
    return order


ORDER = schedule()


def slot_of(node):
    return node[0] * NY + node[1]


def gather_kernel(
    idx, cnt, grads, residual, momentum,
    everyone, acc_out,
    idx_s, cnt_s, idx_v, gbuf, rbuf,
    send_sem, recv_sem, pair_send, pair_recv, in_sem, mom_sem, small_sem,
):
    me = lax.axis_index("dp")
    core = lax.rem(me, 2)
    y = lax.rem(lax.div(me, 2), NY)
    z = lax.div(me, 2 * NY)
    turn = 1 - 2 * core

    def at(dz, dy):
        return (lax.rem(z + turn * dz + NZ, NZ) * NY + lax.rem(y + turn * dy + NY, NY)) * 2 + core

    sibling = me + turn
    targets = {step: at(*step) for step in STEPS}

    barrier = pltpu.get_barrier_semaphore()
    for t in [at(-dz, -dy) for dz, dy in STEPS] + [sibling]:
        pl.semaphore_signal(barrier, inc=1, device_id={"dp": t}, device_id_type=MESH)

    nb = residual.shape[2]
    part = nb // CHUNKS
    small = [
        pltpu.make_async_copy(idx, idx_v, small_sem.at[0]),
        pltpu.make_async_copy(idx, idx_s, small_sem.at[1]),
        pltpu.make_async_copy(cnt, cnt_s, small_sem.at[2]),
    ]
    for b in range(2):
        small.append(
            pltpu.make_async_copy(
                momentum.at[b, :, 0], everyone.at[0, 0, pl.ds(64 * b, 63)], mom_sem.at[b]
            )
        )
    for copy in small:
        copy.start()
    loads = []
    for b in range(2):
        for k in range(CHUNKS):
            span = pl.ds(k * part, part)
            j = b * CHUNKS + k
            g = pltpu.make_async_copy(grads.at[0, b, span], gbuf.at[b, span], in_sem.at[0, j])
            r = pltpu.make_async_copy(residual.at[0, b, span], rbuf.at[b, span], in_sem.at[1, j])
            g.start()
            r.start()
            loads.append((g, r))
    for copy in small:
        copy.wait()
    offset = PITCH * lax.broadcasted_iota(jnp.int32, (2, 16), 0)
    lists = (idx_v[0] + offset).astype(jnp.float32)
    for q in range(8):
        everyone[0, 0, 63:64, 16 * q : 16 * q + 16] = lists[q % 2 : q % 2 + 1]
    lane = lax.broadcasted_iota(jnp.int32, (1, 128), 1)
    own = lax.div(lane, 32) == lax.rem(me, 4)
    everyone[0, 0, 63:64, :] = jnp.where(own, everyone[0, 0, 63:64, :], jnp.float32(0.0))
    everyone[0, 0, 127:128, :] = jnp.zeros((1, 128), jnp.float32)

    def piece(f, node, side=0):
        first, last = FLOWS[f][:2]
        return everyone.at[side, slot_of(node), pl.ds(first, last - first)]

    def remote(src, dst, sent, received, target):
        return pltpu.make_async_remote_copy(
            src_ref=src,
            dst_ref=dst,
            send_sem=sent,
            recv_sem=received,
            device_id={"dp": target},
            device_id_type=MESH,
        )

    def hop(f, node, kid):
        return remote(
            piece(f, node),
            piece(f, kid),
            send_sem.at[f],
            recv_sem.at[f, slot_of(kid)],
            targets[step_of(node, kid)],
        )

    def across(f, node):
        return remote(piece(f, node), piece(f, node, 1), pair_send.at[f], pair_recv.at[f], sibling)

    pl.semaphore_wait(barrier, len(STEPS) + 1)

    def pass_on(f, node, kids):
        for kid in kids:
            hop(f, node, kid).start()
        across(f, node).start()

    for f, node, kids in ORDER:
        if node == (0, 0) and not FLOWS[f][5]:
            pass_on(f, node, kids)
    for b in range(2):
        for k in range(CHUNKS):
            j = b * CHUNKS + k
            span = pl.ds(k * part, part)
            g, r = loads[j]
            g.wait()
            r.wait()
            acc_out[b, span, :] = rbuf[b, span, :] + gbuf[b, span, :].astype(jnp.float32)
    for b in range(2):
        for i in range(16):
            row = acc_out[b, pl.ds(idx_s[0, b, i], 1), :]
            everyone[0, 0, pl.ds(128 + 16 * b + i, 1), :] = jnp.where(
                i < cnt_s[0, b], row, jnp.float32(0.0)
            )
    for f, node, kids in ORDER:
        if node == (0, 0) and FLOWS[f][5]:
            pass_on(f, node, kids)
    parent = {(f, kid): node for f, node, kids in ORDER for kid in kids}
    for f, node, kids in ORDER:
        if node != (0, 0):
            hop(f, parent[(f, node)], node).wait_recv()
            pass_on(f, node, kids)
    for f in range(len(FLOWS)):
        first, last = FLOWS[f][:2]
        span = pl.ds(first, last - first)
        others = everyone.at[0, pl.ds(1, SLOTS - 1), span]
        remote(others, others, send_sem.at[f], pair_recv.at[f], sibling).wait_send()
        pair = remote(everyone.at[0, :, span], everyone.at[1, :, span], pair_send.at[f], pair_recv.at[f], sibling)
        pair.wait_send()
        pair.wait_recv()


def update_kernel(
    sizes, idx_own, cnt, everyone, acc, params,
    new_residual, new_momentum, new_params,
    pbuf, nm, mine_v, lists_v, lists_s, zero_row, mom_sem, res_sem, row_sem, out_sem, list_sem,
):
    me = lax.axis_index("dp")
    core = lax.rem(me, 2)
    y = lax.rem(lax.div(me, 2), NY)
    z = lax.div(me, 2 * NY)
    nb = params.shape[1]
    move = pltpu.make_async_copy(acc, new_residual.at[0], res_sem)
    move.start()
    zero_row[...] = jnp.zeros_like(zero_row)

    def place_of(o):
        oz, oy, oc = o >> 3, (o >> 1) & 3, o & 1
        turn = 1 - 2 * oc
        slot = ((turn * (z - oz)) & (NZ - 1)) * NY + ((turn * (y - oy)) & (NY - 1))
        return (oc + core) & 1, slot

    for q in range(16):
        row = None
        for o in range(4 * q, 4 * q + 4):
            side, slot = place_of(o)
            one = everyone[side, slot, 63:64, :]
            row = one if row is None else row + one
        lists_v[q : q + 1, :] = row.astype(jnp.int32)
    fetch = pltpu.make_async_copy(lists_v, lists_s, list_sem)
    fetch.start()

    def place(o, carry):
        s0, s1, m0, m1 = carry
        side, slot = place_of(o)
        nm[pl.ds(s0, 64), :] = decay_rate * everyone[side, slot, 0:64, :]
        nm[pl.ds(s1, 64), :] = decay_rate * everyone[side, slot, 64:128, :]
        m0 = jnp.where(o == me, s0, m0)
        m1 = jnp.where(o == me, s1, m1)
        return s0 + sizes[0, o], s1 + sizes[1, o], m0, m1

    zero = jnp.int32(0)
    _, _, m0, m1 = lax.fori_loop(0, 64, place, (zero, zero + PITCH, zero, zero), unroll=4)
    fetch.wait()

    def add(q, carry):
        for k in range(4):
            side, slot = place_of(4 * q + k)
            for first in (0, 16):
                rows = []
                for i in range(first, first + 16):
                    j = lists_s[q, 32 * k + i]
                    rows.append((j, nm[pl.ds(j, 1), :] + everyone[side, slot, pl.ds(128 + i, 1), :]))
                for j, row in rows:
                    nm[pl.ds(j, 1), :] = row
        return carry

    lax.fori_loop(0, 16, add, 0)
    part = nb // CHUNKS
    outs = []
    for b in range(2):
        for k in range(CHUNKS):
            span = pl.ds(k * part, part)
            pbuf[b, span, :] = params[b, span, :] - learn_rate * nm[pl.ds(b * PITCH + k * part, part), :]
            out = pltpu.make_async_copy(pbuf.at[b, span], new_params.at[b, span], out_sem.at[b * CHUNKS + k])
            out.start()
            outs.append(out)
    rows = new_momentum.shape[1]
    for b, first in ((0, m0), (1, m1)):
        mine = nm[pl.ds(first, rows), :]
        inside = lax.broadcasted_iota(jnp.int32, (rows, 128), 0) < sizes[b, me]
        mine_v[b] = jnp.where(inside, mine, jnp.float32(0.0))
        out = pltpu.make_async_copy(mine_v.at[b], new_momentum.at[b, :, 0], mom_sem.at[b])
        out.start()
        outs.append(out)
    move.wait()

    def clear(b, i):
        return pltpu.make_async_copy(
            zero_row, new_residual.at[0, b, pl.ds(idx_own[0, b, i], 1)], row_sem.at[b, i]
        )

    for b in range(2):
        for i in range(16):

            @pl.when(i < cnt[0, b])
            def _():
                clear(b, i).start()

    for b in range(2):
        for i in range(16):

            @pl.when(i < cnt[0, b])
            def _():
                clear(b, i).wait()

    for out in outs:
        out.wait()


def on_device(grads, residual, params, momentum, indices, counts, region_sizes):
    nb = grads.shape[2]
    hbm = pl.BlockSpec(memory_space=pltpu.HBM)
    any_space = pl.BlockSpec(memory_space=pl.ANY)
    vmem = pl.BlockSpec(memory_space=pltpu.VMEM)
    smem = pl.BlockSpec(memory_space=pltpu.SMEM)
    dma = pltpu.SemaphoreType.DMA
    everyone, acc = pl.pallas_call(
        gather_kernel,
        out_shape=(
            jax.ShapeDtypeStruct((2, SLOTS, ROWS, 128), jnp.float32),
            jax.ShapeDtypeStruct((2, nb, 128), jnp.float32),
        ),
        in_specs=[hbm] * 5,
        out_specs=(vmem, vmem),
        scratch_shapes=[
            pltpu.SMEM(indices.shape, jnp.int32),
            pltpu.SMEM(counts.shape, jnp.int32),
            pltpu.VMEM(indices.shape, jnp.int32),
            pltpu.VMEM((2, nb, 128), jnp.bfloat16),
            pltpu.VMEM((2, nb, 128), jnp.float32),
            dma((len(FLOWS),)),
            dma((len(FLOWS), SLOTS)),
            dma((len(FLOWS),)),
            dma((len(FLOWS),)),
            dma((2, 2 * CHUNKS)),
            dma((2,)),
            dma((3,)),
        ],
        compiler_params=pltpu.CompilerParams(
            collective_id=0, has_side_effects=True, vmem_limit_bytes=32 << 20
        ),
        name="gather",
    )(*(pltpu.with_memory_space_constraint(a, pltpu.HBM) for a in (indices, counts, grads, residual, jnp.swapaxes(momentum, 1, 2))))
    rows = momentum.shape[2]
    new_residual, new_momentum, new_params = pl.pallas_call(
        update_kernel,
        out_shape=(
            jax.ShapeDtypeStruct((1, 2, nb, 128), jnp.float32),
            jax.ShapeDtypeStruct((2, rows, 1, 128), jnp.float32),
            jax.ShapeDtypeStruct(params.shape, jnp.float32),
        ),
        in_specs=[smem, smem, smem, vmem, vmem, vmem],
        out_specs=(any_space, any_space, any_space),
        scratch_shapes=[
            pltpu.VMEM((2, nb, 128), jnp.float32),
            pltpu.VMEM((2 * PITCH, 128), jnp.float32),
            pltpu.VMEM((2, rows, 128), jnp.float32),
            pltpu.VMEM((16, 128), jnp.int32),
            pltpu.SMEM((16, 128), jnp.int32),
            pltpu.VMEM((1, 128), jnp.float32),
            dma((2,)),
            dma,
            dma((2, 16)),
            dma((2 * CHUNKS,)),
            dma,
        ],
        compiler_params=pltpu.CompilerParams(vmem_limit_bytes=32 << 20),
        name="update",
    )(region_sizes, indices, counts, everyone, acc, params)
    return new_residual, jnp.swapaxes(new_momentum, 1, 2), new_params


def solution(mesh):
    placed = (
        P("dp", "grp", None, None),
        P("dp", "grp", None, None),
        P("grp", None, None),
        P("grp", "dp", None, None),
        P("dp", "grp", None),
        P("dp", "grp"),
        P("grp", None),
    )
    return jax.shard_map(
        on_device,
        mesh=mesh,
        in_specs=placed,
        out_specs=(P("dp", "grp", None, None), P("grp", "dp", None, None), P("grp", None, None)),
        check_vma=False,
    )
```

```python
import functools
import heapq

import jax
import jax.numpy as jnp
from jax import lax
from jax.experimental import pallas as pl
from jax.experimental.pallas import tpu as pltpu
from jax.sharding import PartitionSpec as P

decay_rate = 0.9
learn_rate = 0.1

NZ, NY = 8, 4
SLOTS = NZ * NY
ROWS = 160
MESH = pl.DeviceIdType.MESH
CHUNKS = 4
TILE = 256
PICKED = 128
PITCH = 2048 + 64


FLOWS = (
    (0, 120, (0, 0, 3, 0, 0, 4, 10, 11, 4, 5, 11, 8, 8, 9, 15, 11, 24, 21, 26, 16, 16, 25, 21, 19, 0, 24, 27, 24, 31, 1, 29, 30)),
    (120, 160, (0, 0, 1, 0, 0, 4, 5, 4, 4, 5, 6, 7, 0, 12, 13, 12, 24, 16, 19, 16, 24, 29, 21, 20, 0, 24, 27, 31, 0, 28, 2, 3)),
)


def tree_of(flow):
    children = {(rz, ry): [] for rz in range(NZ) for ry in range(NY)}
    for slot, parent in enumerate(flow[2]):
        if slot:
            children[divmod(parent, NY)].append(divmod(slot, NY))
    return children


TREES = tuple(tree_of(flow) for flow in FLOWS)


def step_of(node, kid):
    dz, dy = (kid[0] - node[0]) % NZ, (kid[1] - node[1]) % NY
    return (dz if 2 * dz <= NZ else dz - NZ), (dy if 2 * dy <= NY else dy - NY)


STEPS = tuple(sorted({step_of(n, k) for t in TREES for n, kids in t.items() for k in kids}))
LATENCY, PER_HOP, PICKS = 1.6, 0.65, 1.5


def schedule():
    def height(f, node):
        return 1 + max((height(f, c) for c in TREES[f][node]), default=0)

    heap = [(PICKS if (FLOWS[f][1] > PICKED) else 0.0, f, (0, 0)) for f in range(len(FLOWS))]
    free = {"z": 0.0, "y": 0.0}
    now, order = 0.0, []
    while heap:
        at, f, node = heapq.heappop(heap)
        now = max(now, at) + 0.05
        kids = sorted(TREES[f][node], key=lambda c: -height(f, c))
        order.append((f, node, kids))
        for kid in kids:
            now += 0.07
            dz, dy = step_of(node, kid)
            axis, hops = ("z", abs(dz)) if dz else ("y", abs(dy))
            free[axis] = max(free[axis], now) + hops * (FLOWS[f][1] - FLOWS[f][0]) * 512 / 105e3
            heapq.heappush(heap, (free[axis] + LATENCY + hops * PER_HOP, f, kid))
    return order


ORDER = schedule()


def slot_of(node):
    return node[0] * NY + node[1]


def gather_kernel(
    idx, cnt, grads, residual, momentum,
    everyone, acc_out, total,
    idx_s, cnt_s, idx_v, gbuf, rbuf, keys, halves,
    send_sem, recv_sem, pair_send, pair_recv, in_sem, mom_sem, small_sem,
):
    me = lax.axis_index("dp")
    core = lax.rem(me, 2)
    y = lax.rem(lax.div(me, 2), NY)
    z = lax.div(me, 2 * NY)
    turn = 1 - 2 * core

    def at(dz, dy):
        return (lax.rem(z + turn * dz + NZ, NZ) * NY + lax.rem(y + turn * dy + NY, NY)) * 2 + core

    sibling = me + turn
    targets = {step: at(*step) for step in STEPS}

    barrier = pltpu.get_barrier_semaphore()
    for t in [at(-dz, -dy) for dz, dy in STEPS] + [sibling]:
        pl.semaphore_signal(barrier, inc=1, device_id={"dp": t}, device_id_type=MESH)

    nb = residual.shape[2]
    part = nb // CHUNKS
    small = [
        pltpu.make_async_copy(idx, idx_v, small_sem.at[0]),
        pltpu.make_async_copy(idx, idx_s, small_sem.at[1]),
        pltpu.make_async_copy(cnt, cnt_s, small_sem.at[2]),
    ]
    for b in range(2):
        small.append(
            pltpu.make_async_copy(
                momentum.at[b, :, 0], everyone.at[0, 0, pl.ds(63 * b, 63)], mom_sem.at[b]
            )
        )
    for copy in small:
        copy.start()
    loads = []
    for b in range(2):
        for k in range(CHUNKS):
            span = pl.ds(k * part, part)
            j = b * CHUNKS + k
            g = pltpu.make_async_copy(grads.at[0, b, span], gbuf.at[b, span], in_sem.at[0, j])
            r = pltpu.make_async_copy(residual.at[0, b, span], rbuf.at[b, span], in_sem.at[1, j])
            g.start()
            r.start()
            loads.append((g, r))
    for copy in small:
        copy.wait()
    lists = idx_v[0].astype(jnp.float32)
    lane = lax.broadcasted_iota(jnp.int32, (1, 128), 1)
    own = lax.div(lane, 16) == lax.rem(z, 2) * NY + y
    for b in range(2):
        at_row = pl.ds(126 + b, 1)
        for q in range(8):
            everyone[0, 0, at_row, 16 * q : 16 * q + 16] = lists[b : b + 1]
        everyone[0, 0, at_row, :] = jnp.where(own, everyone[0, 0, at_row, :], jnp.float32(0.0))

    def piece(f, node, side=0):
        first, last = FLOWS[f][:2]
        return everyone.at[side, slot_of(node), pl.ds(first, last - first)]

    def remote(src, dst, sent, received, target):
        return pltpu.make_async_remote_copy(
            src_ref=src,
            dst_ref=dst,
            send_sem=sent,
            recv_sem=received,
            device_id={"dp": target},
            device_id_type=MESH,
        )

    def hop(f, node, kid):
        return remote(
            piece(f, node),
            piece(f, kid),
            send_sem.at[f],
            recv_sem.at[f, slot_of(kid)],
            targets[step_of(node, kid)],
        )

    def across(f, node):
        return remote(piece(f, node), piece(f, node, 1), pair_send.at[f], pair_recv.at[f], sibling)

    pl.semaphore_wait(barrier, len(STEPS) + 1)

    def pass_on(f, node, kids):
        for kid in kids:
            hop(f, node, kid).start()
        across(f, node).start()

    for f, node, kids in ORDER:
        if node == (0, 0) and not (FLOWS[f][1] > PICKED):
            pass_on(f, node, kids)
    for b in range(2):
        for k in range(CHUNKS):
            j = b * CHUNKS + k
            span = pl.ds(k * part, part)
            g, r = loads[j]
            g.wait()
            r.wait()
            acc_out[b, span, :] = rbuf[b, span, :] + gbuf[b, span, :].astype(jnp.float32)
    for b in range(2):
        for i in range(16):
            row = acc_out[b, pl.ds(idx_s[0, b, i], 1), :]
            everyone[0, 0, pl.ds(128 + 16 * b + i, 1), :] = jnp.where(
                i < cnt_s[0, b], row, jnp.float32(0.0)
            )
    for f, node, kids in ORDER:
        if node == (0, 0) and (FLOWS[f][1] > PICKED):
            pass_on(f, node, kids)
    def collect():
        for side in range(2):
            way = turn if side == 0 else -turn
            for pair in range(NZ // 2):
                group = side * (NZ // 2) + pair
                sums = [None, None]
                for p in range(8):
                    rz = 2 * pair + lax.rem(z + p // NY, 2)
                    ry = lax.rem(way * (y - p % NY) + NY, NY)
                    slot = rz * NY + ry
                    for b in range(2):
                        row = everyone[side, slot, pl.ds(126 + b, 1), :]
                        sums[b] = row if sums[b] is None else sums[b] + row
                        block = everyone[side, slot, pl.ds(PICKED + 16 * b, 16), :]
                        high = block.astype(jnp.bfloat16)
                        low = (block - high.astype(jnp.float32)).astype(jnp.bfloat16)
                        k = pl.ds(128 * group + 16 * p, 16)
                        halves[b, k, 0:128] = high
                        halves[b, k, 128:256] = low
                for b in range(2):
                    keys[b, :, pl.ds(128 * group, 128)] = sums[b].astype(jnp.int32)

    def sum_tile(t):
        b, first = divmod(t * TILE, nb)
        row = lax.broadcasted_iota(jnp.int32, (TILE, 1024), 0) + first
        hit = (row == keys[b]).astype(jnp.float32).astype(jnp.bfloat16)
        both = jnp.dot(hit, halves[b], preferred_element_type=jnp.float32)
        total[b, pl.ds(first, TILE), :] = both[:, 0:128] + both[:, 128:256]

    def settle(f):
        first, last = FLOWS[f][:2]
        span = pl.ds(first, last - first)
        others = everyone.at[0, pl.ds(1, SLOTS - 1), span]
        remote(others, others, send_sem.at[f], pair_recv.at[f], sibling).wait_send()
        pair = remote(everyone.at[0, :, span], everyone.at[1, :, span], pair_send.at[f], pair_recv.at[f], sibling)
        pair.wait_send()
        pair.wait_recv()

    parent = {(f, kid): node for f, node, kids in ORDER for kid in kids}
    later = [entry for entry in ORDER if entry[1] != (0, 0)]
    collected = max(n for n, entry in enumerate(later) if entry[0] == len(FLOWS) - 1)
    for n, (f, node, kids) in enumerate(later):
        hop(f, parent[(f, node)], node).wait_recv()
        pass_on(f, node, kids)
        if n == collected:
            settle(len(FLOWS) - 1)
            collect()
    for t in range(2 * nb // TILE):
        sum_tile(t)
    for f in range(len(FLOWS) - 1):
        settle(f)


def update_kernel(
    sizes, idx_own, cnt, everyone, acc, total, params,
    new_residual, new_momentum, new_params,
    pbuf, nm, mine_v, zero_row, mom_sem, res_sem, row_sem, out_sem,
):
    me = lax.axis_index("dp")
    core = lax.rem(me, 2)
    y = lax.rem(lax.div(me, 2), NY)
    z = lax.div(me, 2 * NY)
    nb = params.shape[1]
    moves = [pltpu.make_async_copy(acc.at[b], new_residual.at[0, b], res_sem.at[b]) for b in range(2)]
    for move in moves:
        move.start()
    zero_row[...] = jnp.zeros_like(zero_row)

    def place_of(o):
        oz, oy, oc = o >> 3, (o >> 1) & 3, o & 1
        turn = 1 - 2 * oc
        slot = ((turn * (z - oz)) & (NZ - 1)) * NY + ((turn * (y - oy)) & (NY - 1))
        return (oc + core) & 1, slot

    part = nb // CHUNKS
    rows = new_momentum.shape[1]
    outs = []
    for b in range(2):

        def place(o, carry):
            start, mine = carry
            side, slot = place_of(o)
            nm[b, pl.ds(start, 64), :] = decay_rate * everyone[side, slot, 63 * b : 63 * b + 64, :]
            return start + sizes[b, o], jnp.where(o == me, start, mine)

        _, first = lax.fori_loop(0, 64, place, (jnp.int32(0), jnp.int32(0)), unroll=8)
        for k in range(CHUNKS):
            span = pl.ds(k * part, part)
            pbuf[b, span, :] = params[b, span, :] - learn_rate * (nm[b, span, :] + total[b, span, :])
            out = pltpu.make_async_copy(pbuf.at[b, span], new_params.at[b, span], out_sem.at[b * CHUNKS + k])
            out.start()
            outs.append(out)
        window = pl.ds(first, rows)
        inside = lax.broadcasted_iota(jnp.int32, (rows, 128), 0) < sizes[b, me]
        mine_v[b] = jnp.where(inside, nm[b, window, :] + total[b, window, :], jnp.float32(0.0))
        out = pltpu.make_async_copy(mine_v.at[b], new_momentum.at[b, :, 0], mom_sem.at[b])
        out.start()
        outs.append(out)

    def clear(b, i):
        return pltpu.make_async_copy(
            zero_row, new_residual.at[0, b, pl.ds(idx_own[0, b, i], 1)], row_sem.at[b, i]
        )

    for b in range(2):
        moves[b].wait()
        for i in range(16):

            @pl.when(i < cnt[0, b])
            def _():
                clear(b, i).start()

    for b in range(2):
        for i in range(16):

            @pl.when(i < cnt[0, b])
            def _():
                clear(b, i).wait()

    for out in outs:
        out.wait()


def on_device(grads, residual, params, momentum, indices, counts, region_sizes):
    nb = grads.shape[2]
    hbm = pl.BlockSpec(memory_space=pltpu.HBM)
    any_space = pl.BlockSpec(memory_space=pl.ANY)
    vmem = pl.BlockSpec(memory_space=pltpu.VMEM)
    smem = pl.BlockSpec(memory_space=pltpu.SMEM)
    dma = pltpu.SemaphoreType.DMA
    everyone, acc, total = pl.pallas_call(
        gather_kernel,
        out_shape=(
            jax.ShapeDtypeStruct((2, SLOTS, ROWS, 128), jnp.float32),
            jax.ShapeDtypeStruct((2, nb, 128), jnp.float32),
            jax.ShapeDtypeStruct((2, PITCH, 128), jnp.float32),
        ),
        in_specs=[hbm] * 5,
        out_specs=(vmem, vmem, vmem),
        scratch_shapes=[
            pltpu.SMEM(indices.shape, jnp.int32),
            pltpu.SMEM(counts.shape, jnp.int32),
            pltpu.VMEM(indices.shape, jnp.int32),
            pltpu.VMEM((2, nb, 128), jnp.bfloat16),
            pltpu.VMEM((2, nb, 128), jnp.float32),
            pltpu.VMEM((2, 1, 1024), jnp.int32),
            pltpu.VMEM((2, 1024, 256), jnp.bfloat16),
            dma((len(FLOWS),)),
            dma((len(FLOWS), SLOTS)),
            dma((len(FLOWS),)),
            dma((len(FLOWS),)),
            dma((2, 2 * CHUNKS)),
            dma((2,)),
            dma((3,)),
        ],
        compiler_params=pltpu.CompilerParams(
            collective_id=0, has_side_effects=True, vmem_limit_bytes=32 << 20
        ),
        name="gather",
    )(*(pltpu.with_memory_space_constraint(a, pltpu.HBM) for a in (indices, counts, grads, residual, jnp.swapaxes(momentum, 1, 2))))
    rows = momentum.shape[2]
    new_residual, new_momentum, new_params = pl.pallas_call(
        update_kernel,
        out_shape=(
            jax.ShapeDtypeStruct((1, 2, nb, 128), jnp.float32),
            jax.ShapeDtypeStruct((2, rows, 1, 128), jnp.float32),
            jax.ShapeDtypeStruct(params.shape, jnp.float32),
        ),
        in_specs=[smem, smem, smem, vmem, vmem, vmem, vmem],
        out_specs=(any_space, any_space, any_space),
        scratch_shapes=[
            pltpu.VMEM((2, nb, 128), jnp.float32),
            pltpu.VMEM((2, PITCH, 128), jnp.float32),
            pltpu.VMEM((2, rows, 128), jnp.float32),
            pltpu.VMEM((1, 128), jnp.float32),
            dma((2,)),
            dma((2,)),
            dma((2, 16)),
            dma((2 * CHUNKS,)),
        ],
        compiler_params=pltpu.CompilerParams(vmem_limit_bytes=32 << 20),
        name="update",
    )(region_sizes, indices, counts, everyone, acc, total, params)
    return new_residual, jnp.swapaxes(new_momentum, 1, 2), new_params


def solution(mesh):
    placed = (
        P("dp", "grp", None, None),
        P("dp", "grp", None, None),
        P("grp", None, None),
        P("grp", "dp", None, None),
        P("dp", "grp", None),
        P("dp", "grp"),
        P("grp", None),
    )
    return jax.shard_map(
        on_device,
        mesh=mesh,
        in_specs=placed,
        out_specs=(P("dp", "grp", None, None), P("grp", "dp", None, None), P("grp", None, None)),
        check_vma=False,
    )
```

```python
import functools
import heapq

import jax
import jax.numpy as jnp
from jax import lax
from jax.experimental import pallas as pl
from jax.experimental.pallas import tpu as pltpu
from jax.sharding import PartitionSpec as P

decay_rate = 0.9
learn_rate = 0.1

NZ, NY = 8, 4
SLOTS = NZ * NY
ROWS = 160
MESH = pl.DeviceIdType.MESH
CHUNKS = 4
TILE = 256
PICKED = 128
PITCH = 2048 + 64


FLOWS = (
    (0, 80, (0, 0, 22, 0, 0, 4, 5, 3, 4, 13, 6, 7, 8, 12, 15, 12, 12, 16, 22, 16, 23, 20, 23, 3, 20, 24, 22, 31, 0, 28, 31, 28)),
    (80, 160, (0, 0, 0, 2, 5, 6, 2, 6, 0, 8, 8, 10, 8, 12, 10, 12, 24, 16, 26, 18, 12, 20, 26, 20, 0, 24, 2, 31, 0, 28, 31, 28)),
)


def tree_of(flow):
    children = {(rz, ry): [] for rz in range(NZ) for ry in range(NY)}
    for slot, parent in enumerate(flow[2]):
        if slot:
            children[divmod(parent, NY)].append(divmod(slot, NY))
    return children


TREES = tuple(tree_of(flow) for flow in FLOWS)


def step_of(node, kid):
    dz, dy = (kid[0] - node[0]) % NZ, (kid[1] - node[1]) % NY
    return (dz if 2 * dz <= NZ else dz - NZ), (dy if 2 * dy <= NY else dy - NY)


STEPS = tuple(sorted({step_of(n, k) for t in TREES for n, kids in t.items() for k in kids}))
LATENCY, PER_HOP, PICKS = 1.6, 0.65, 1.5


def schedule():
    def height(f, node):
        return 1 + max((height(f, c) for c in TREES[f][node]), default=0)

    heap = [(PICKS if (FLOWS[f][1] > PICKED) else 0.0, f, (0, 0)) for f in range(len(FLOWS))]
    free = {"z": 0.0, "y": 0.0}
    now, order = 0.0, []
    while heap:
        at, f, node = heapq.heappop(heap)
        now = max(now, at) + 0.05
        kids = sorted(TREES[f][node], key=lambda c: -height(f, c))
        order.append((f, node, kids))
        for kid in kids:
            now += 0.07
            dz, dy = step_of(node, kid)
            axis, hops = ("z", abs(dz)) if dz else ("y", abs(dy))
            free[axis] = max(free[axis], now) + hops * (FLOWS[f][1] - FLOWS[f][0]) * 512 / 105e3
            heapq.heappush(heap, (free[axis] + LATENCY + hops * PER_HOP, f, kid))
    return order


ORDER = schedule()


def slot_of(node):
    return node[0] * NY + node[1]


def gather_kernel(
    idx, cnt, grads, residual, momentum,
    everyone, acc_out, total,
    idx_s, cnt_s, idx_v, gbuf, rbuf, keys, halves,
    send_sem, recv_sem, pair_send, pair_recv, in_sem, mom_sem, small_sem,
):
    me = lax.axis_index("dp")
    core = lax.rem(me, 2)
    y = lax.rem(lax.div(me, 2), NY)
    z = lax.div(me, 2 * NY)
    turn = 1 - 2 * core

    def at(dz, dy):
        return (lax.rem(z + turn * dz + NZ, NZ) * NY + lax.rem(y + turn * dy + NY, NY)) * 2 + core

    sibling = me + turn
    targets = {step: at(*step) for step in STEPS}

    barrier = pltpu.get_barrier_semaphore()
    for t in [at(-dz, -dy) for dz, dy in STEPS] + [sibling]:
        pl.semaphore_signal(barrier, inc=1, device_id={"dp": t}, device_id_type=MESH)

    nb = residual.shape[2]
    part = nb // CHUNKS
    small = [
        pltpu.make_async_copy(idx, idx_v, small_sem.at[0]),
        pltpu.make_async_copy(idx, idx_s, small_sem.at[1]),
        pltpu.make_async_copy(cnt, cnt_s, small_sem.at[2]),
    ]
    for b in range(2):
        small.append(
            pltpu.make_async_copy(
                momentum.at[b, :, 0], everyone.at[0, 0, pl.ds(63 * b, 63)], mom_sem.at[b]
            )
        )
    for copy in small:
        copy.start()
    loads = []
    for b in range(2):
        for k in range(CHUNKS):
            span = pl.ds(k * part, part)
            j = b * CHUNKS + k
            g = pltpu.make_async_copy(grads.at[0, b, span], gbuf.at[b, span], in_sem.at[0, j])
            r = pltpu.make_async_copy(residual.at[0, b, span], rbuf.at[b, span], in_sem.at[1, j])
            g.start()
            r.start()
            loads.append((g, r))
    for copy in small:
        copy.wait()
    lists = idx_v[0].astype(jnp.float32)
    lane = lax.broadcasted_iota(jnp.int32, (1, 128), 1)
    own = lax.div(lane, 16) == lax.rem(z, 2) * NY + y
    for b in range(2):
        at_row = pl.ds(126 + b, 1)
        for q in range(8):
            everyone[0, 0, at_row, 16 * q : 16 * q + 16] = lists[b : b + 1]
        everyone[0, 0, at_row, :] = jnp.where(own, everyone[0, 0, at_row, :], jnp.float32(0.0))

    def piece(f, node, side=0):
        first, last = FLOWS[f][:2]
        return everyone.at[side, slot_of(node), pl.ds(first, last - first)]

    def remote(src, dst, sent, received, target):
        return pltpu.make_async_remote_copy(
            src_ref=src,
            dst_ref=dst,
            send_sem=sent,
            recv_sem=received,
            device_id={"dp": target},
            device_id_type=MESH,
        )

    def hop(f, node, kid):
        return remote(
            piece(f, node),
            piece(f, kid),
            send_sem.at[f],
            recv_sem.at[f, slot_of(kid)],
            targets[step_of(node, kid)],
        )

    def across(f, node):
        return remote(piece(f, node), piece(f, node, 1), pair_send.at[f], pair_recv.at[f], sibling)

    pl.semaphore_wait(barrier, len(STEPS) + 1)

    def pass_on(f, node, kids):
        for kid in kids:
            hop(f, node, kid).start()
        across(f, node).start()

    for f, node, kids in ORDER:
        if node == (0, 0) and not (FLOWS[f][1] > PICKED):
            pass_on(f, node, kids)
    for b in range(2):
        for k in range(CHUNKS):
            j = b * CHUNKS + k
            span = pl.ds(k * part, part)
            g, r = loads[j]
            g.wait()
            r.wait()
            acc_out[b, span, :] = rbuf[b, span, :] + gbuf[b, span, :].astype(jnp.float32)
    for b in range(2):
        for i in range(16):
            row = acc_out[b, pl.ds(idx_s[0, b, i], 1), :]
            everyone[0, 0, pl.ds(128 + 16 * b + i, 1), :] = jnp.where(
                i < cnt_s[0, b], row, jnp.float32(0.0)
            )
    for f, node, kids in ORDER:
        if node == (0, 0) and (FLOWS[f][1] > PICKED):
            pass_on(f, node, kids)
    def collect(side):
        way = turn if side == 0 else -turn
        for pair in range(NZ // 2):
            group = side * (NZ // 2) + pair
            sums = [None, None]
            for p in range(8):
                rz = 2 * pair + lax.rem(z + p // NY, 2)
                ry = lax.rem(way * (y - p % NY) + NY, NY)
                slot = rz * NY + ry
                for b in range(2):
                    row = everyone[side, slot, pl.ds(126 + b, 1), :]
                    sums[b] = row if sums[b] is None else sums[b] + row
                    block = everyone[side, slot, pl.ds(PICKED + 16 * b, 16), :]
                    high = block.astype(jnp.bfloat16)
                    low = (block - high.astype(jnp.float32)).astype(jnp.bfloat16)
                    k = pl.ds(128 * group + 16 * p, 16)
                    halves[b, k, 0:128] = high
                    halves[b, k, 128:256] = low
            for b in range(2):
                keys[b, :, pl.ds(128 * group, 128)] = sums[b].astype(jnp.int32)

    def sum_tile(t, side):
        b, first = divmod(t * TILE, nb)
        k = pl.ds(512 * side, 512)
        row = lax.broadcasted_iota(jnp.int32, (TILE, 512), 0) + first
        hit = (row == keys[b, :, k]).astype(jnp.float32).astype(jnp.bfloat16)
        both = jnp.dot(hit, halves[b, k, :], preferred_element_type=jnp.float32)
        tile = both[:, 0:128] + both[:, 128:256]
        if side:
            tile = tile + total[b, pl.ds(first, TILE), :]
        total[b, pl.ds(first, TILE), :] = tile

    def settle(f):
        first, last = FLOWS[f][:2]
        span = pl.ds(first, last - first)
        others = everyone.at[0, pl.ds(1, SLOTS - 1), span]
        remote(others, others, send_sem.at[f], pair_recv.at[f], sibling).wait_send()
        pair = remote(everyone.at[0, :, span], everyone.at[1, :, span], pair_send.at[f], pair_recv.at[f], sibling)
        pair.wait_send()
        pair.wait_recv()

    parent = {(f, kid): node for f, node, kids in ORDER for kid in kids}
    later = [entry for entry in ORDER if entry[1] != (0, 0)]
    for f, node, kids in later:
        hop(f, parent[(f, node)], node).wait_recv()
        pass_on(f, node, kids)
    for side in range(2):
        if side:
            settle(len(FLOWS) - 1)
        collect(side)
        for t in range(2 * nb // TILE):
            sum_tile(t, side)
    for f in range(len(FLOWS) - 1):
        settle(f)


def update_kernel(
    sizes, idx_own, cnt, everyone, acc, total, params,
    new_residual, new_momentum, new_params,
    pbuf, nm, mine_v, zero_row, mom_sem, res_sem, row_sem, out_sem,
):
    me = lax.axis_index("dp")
    core = lax.rem(me, 2)
    y = lax.rem(lax.div(me, 2), NY)
    z = lax.div(me, 2 * NY)
    nb = params.shape[1]
    moves = [pltpu.make_async_copy(acc.at[b], new_residual.at[0, b], res_sem.at[b]) for b in range(2)]
    for move in moves:
        move.start()
    zero_row[...] = jnp.zeros_like(zero_row)

    def place_of(o):
        oz, oy, oc = o >> 3, (o >> 1) & 3, o & 1
        turn = 1 - 2 * oc
        slot = ((turn * (z - oz)) & (NZ - 1)) * NY + ((turn * (y - oy)) & (NY - 1))
        return (oc + core) & 1, slot

    part = nb // CHUNKS
    rows = new_momentum.shape[1]
    outs = []
    for b in range(2):

        def place(o, carry):
            start, mine = carry
            side, slot = place_of(o)
            nm[b, pl.ds(start, 64), :] = decay_rate * everyone[side, slot, 63 * b : 63 * b + 64, :]
            return start + sizes[b, o], jnp.where(o == me, start, mine)

        _, first = lax.fori_loop(0, 64, place, (jnp.int32(0), jnp.int32(0)), unroll=8)
        for k in range(CHUNKS):
            span = pl.ds(k * part, part)
            pbuf[b, span, :] = params[b, span, :] - learn_rate * (nm[b, span, :] + total[b, span, :])
            out = pltpu.make_async_copy(pbuf.at[b, span], new_params.at[b, span], out_sem.at[b * CHUNKS + k])
            out.start()
            outs.append(out)
        window = pl.ds(first, rows)
        inside = lax.broadcasted_iota(jnp.int32, (rows, 128), 0) < sizes[b, me]
        mine_v[b] = jnp.where(inside, nm[b, window, :] + total[b, window, :], jnp.float32(0.0))
        out = pltpu.make_async_copy(mine_v.at[b], new_momentum.at[b, :, 0], mom_sem.at[b])
        out.start()
        outs.append(out)

    def clear(b, i):
        return pltpu.make_async_copy(
            zero_row, new_residual.at[0, b, pl.ds(idx_own[0, b, i], 1)], row_sem.at[b, i]
        )

    for b in range(2):
        moves[b].wait()
        for i in range(16):

            @pl.when(i < cnt[0, b])
            def _():
                clear(b, i).start()

    for b in range(2):
        for i in range(16):

            @pl.when(i < cnt[0, b])
            def _():
                clear(b, i).wait()

    for out in outs:
        out.wait()


def on_device(grads, residual, params, momentum, indices, counts, region_sizes):
    nb = grads.shape[2]
    hbm = pl.BlockSpec(memory_space=pltpu.HBM)
    any_space = pl.BlockSpec(memory_space=pl.ANY)
    vmem = pl.BlockSpec(memory_space=pltpu.VMEM)
    smem = pl.BlockSpec(memory_space=pltpu.SMEM)
    dma = pltpu.SemaphoreType.DMA
    everyone, acc, total = pl.pallas_call(
        gather_kernel,
        out_shape=(
            jax.ShapeDtypeStruct((2, SLOTS, ROWS, 128), jnp.float32),
            jax.ShapeDtypeStruct((2, nb, 128), jnp.float32),
            jax.ShapeDtypeStruct((2, PITCH, 128), jnp.float32),
        ),
        in_specs=[hbm] * 5,
        out_specs=(vmem, vmem, vmem),
        scratch_shapes=[
            pltpu.SMEM(indices.shape, jnp.int32),
            pltpu.SMEM(counts.shape, jnp.int32),
            pltpu.VMEM(indices.shape, jnp.int32),
            pltpu.VMEM((2, nb, 128), jnp.bfloat16),
            pltpu.VMEM((2, nb, 128), jnp.float32),
            pltpu.VMEM((2, 1, 1024), jnp.int32),
            pltpu.VMEM((2, 1024, 256), jnp.bfloat16),
            dma((len(FLOWS),)),
            dma((len(FLOWS), SLOTS)),
            dma((len(FLOWS),)),
            dma((len(FLOWS),)),
            dma((2, 2 * CHUNKS)),
            dma((2,)),
            dma((3,)),
        ],
        compiler_params=pltpu.CompilerParams(
            collective_id=0, has_side_effects=True, vmem_limit_bytes=32 << 20
        ),
        name="gather",
    )(*(pltpu.with_memory_space_constraint(a, pltpu.HBM) for a in (indices, counts, grads, residual, jnp.swapaxes(momentum, 1, 2))))
    rows = momentum.shape[2]
    new_residual, new_momentum, new_params = pl.pallas_call(
        update_kernel,
        out_shape=(
            jax.ShapeDtypeStruct((1, 2, nb, 128), jnp.float32),
            jax.ShapeDtypeStruct((2, rows, 1, 128), jnp.float32),
            jax.ShapeDtypeStruct(params.shape, jnp.float32),
        ),
        in_specs=[smem, smem, smem, vmem, vmem, vmem, vmem],
        out_specs=(any_space, any_space, any_space),
        scratch_shapes=[
            pltpu.VMEM((2, nb, 128), jnp.float32),
            pltpu.VMEM((2, PITCH, 128), jnp.float32),
            pltpu.VMEM((2, rows, 128), jnp.float32),
            pltpu.VMEM((1, 128), jnp.float32),
            dma((2,)),
            dma((2,)),
            dma((2, 16)),
            dma((2 * CHUNKS,)),
        ],
        compiler_params=pltpu.CompilerParams(vmem_limit_bytes=32 << 20),
        name="update",
    )(region_sizes, indices, counts, everyone, acc, total, params)
    return new_residual, jnp.swapaxes(new_momentum, 1, 2), new_params


def solution(mesh):
    placed = (
        P("dp", "grp", None, None),
        P("dp", "grp", None, None),
        P("grp", None, None),
        P("grp", "dp", None, None),
        P("dp", "grp", None),
        P("dp", "grp"),
        P("grp", None),
    )
    return jax.shard_map(
        on_device,
        mesh=mesh,
        in_specs=placed,
        out_specs=(P("dp", "grp", None, None), P("grp", "dp", None, None), P("grp", None, None)),
        check_vma=False,
    )
```

```python
import functools
import heapq

import jax
import jax.numpy as jnp
from jax import lax
from jax.experimental import pallas as pl
from jax.experimental.pallas import tpu as pltpu
from jax.sharding import PartitionSpec as P

decay_rate = 0.9
learn_rate = 0.1

NZ, NY = 8, 4
SLOTS = NZ * NY
ROWS = 160
MESH = pl.DeviceIdType.MESH
CHUNKS = 4
TILE = 512
PICKED = 128
PITCH = 2048 + 64


FLOWS = (
    (0, 80, (0, 0, 22, 0, 0, 4, 5, 3, 4, 13, 6, 7, 8, 12, 15, 12, 12, 16, 22, 16, 23, 20, 23, 3, 20, 24, 22, 31, 0, 28, 31, 28)),
    (80, 160, (0, 0, 0, 2, 5, 6, 2, 6, 0, 8, 8, 10, 8, 12, 10, 12, 24, 16, 26, 18, 12, 20, 26, 20, 0, 24, 2, 31, 0, 28, 31, 28)),
)


def tree_of(flow):
    children = {(rz, ry): [] for rz in range(NZ) for ry in range(NY)}
    for slot, parent in enumerate(flow[2]):
        if slot:
            children[divmod(parent, NY)].append(divmod(slot, NY))
    return children


TREES = tuple(tree_of(flow) for flow in FLOWS)


def step_of(node, kid):
    dz, dy = (kid[0] - node[0]) % NZ, (kid[1] - node[1]) % NY
    return (dz if 2 * dz <= NZ else dz - NZ), (dy if 2 * dy <= NY else dy - NY)


STEPS = tuple(sorted({step_of(n, k) for t in TREES for n, kids in t.items() for k in kids}))
LATENCY, PER_HOP, PICKS = 2.0, 0.65, 1.5


def schedule():
    def height(f, node):
        return 1 + max((height(f, c) for c in TREES[f][node]), default=0)

    heap = [(PICKS if (FLOWS[f][1] > PICKED) else 0.0, f, (0, 0)) for f in range(len(FLOWS))]
    free = {"z": 0.0, "y": 0.0}
    now, order = 0.0, []
    while heap:
        at, f, node = heapq.heappop(heap)
        now = max(now, at) + 0.02
        kids = sorted(TREES[f][node], key=lambda c: -height(f, c))
        order.append((f, node, kids))
        for kid in kids:
            now += 0.02
            dz, dy = step_of(node, kid)
            axis, hops = ("z", abs(dz)) if dz else ("y", abs(dy))
            free[axis] = max(free[axis], now) + hops * (FLOWS[f][1] - FLOWS[f][0]) * 512 / 102e3
            heapq.heappush(heap, (free[axis] + LATENCY + hops * PER_HOP, f, kid))
    return order


ORDER = schedule()


def slot_of(node):
    return node[0] * NY + node[1]


def gather_kernel(
    idx, cnt, grads, residual, momentum,
    everyone, acc_out, total,
    idx_s, cnt_s, idx_v, gbuf, rbuf, keys, halves,
    send_sem, recv_sem, pair_send, pair_recv, in_sem, mom_sem, small_sem,
):
    me = lax.axis_index("dp")
    core = lax.rem(me, 2)
    y = lax.rem(lax.div(me, 2), NY)
    z = lax.div(me, 2 * NY)
    turn = 1 - 2 * core

    def at(dz, dy):
        return (lax.rem(z + turn * dz + NZ, NZ) * NY + lax.rem(y + turn * dy + NY, NY)) * 2 + core

    sibling = me + turn
    targets = {step: at(*step) for step in STEPS}

    barrier = pltpu.get_barrier_semaphore()
    for t in [at(-dz, -dy) for dz, dy in STEPS] + [sibling]:
        pl.semaphore_signal(barrier, inc=1, device_id={"dp": t}, device_id_type=MESH)

    nb = residual.shape[2]
    part = nb // CHUNKS
    small = [
        pltpu.make_async_copy(idx, idx_v, small_sem.at[0]),
        pltpu.make_async_copy(idx, idx_s, small_sem.at[1]),
        pltpu.make_async_copy(cnt, cnt_s, small_sem.at[2]),
    ]
    for b in range(2):
        small.append(
            pltpu.make_async_copy(
                momentum.at[b, :, 0], everyone.at[0, 0, pl.ds(63 * b, 63)], mom_sem.at[b]
            )
        )
    for copy in small:
        copy.start()
    loads = []
    for b in range(2):
        for k in range(CHUNKS):
            span = pl.ds(k * part, part)
            j = b * CHUNKS + k
            g = pltpu.make_async_copy(grads.at[0, b, span], gbuf.at[b, span], in_sem.at[0, j])
            r = pltpu.make_async_copy(residual.at[0, b, span], rbuf.at[b, span], in_sem.at[1, j])
            g.start()
            r.start()
            loads.append((g, r))
    for copy in small:
        copy.wait()
    lists = idx_v[0].astype(jnp.float32)
    lane = lax.broadcasted_iota(jnp.int32, (1, 128), 1)
    own = lax.div(lane, 16) == lax.rem(z, 2) * NY + y
    for b in range(2):
        at_row = pl.ds(126 + b, 1)
        for q in range(8):
            everyone[0, 0, at_row, 16 * q : 16 * q + 16] = lists[b : b + 1]
        everyone[0, 0, at_row, :] = jnp.where(own, everyone[0, 0, at_row, :], jnp.float32(0.0))

    def piece(f, node, side=0):
        first, last = FLOWS[f][:2]
        return everyone.at[side, slot_of(node), pl.ds(first, last - first)]

    def remote(src, dst, sent, received, target):
        return pltpu.make_async_remote_copy(
            src_ref=src,
            dst_ref=dst,
            send_sem=sent,
            recv_sem=received,
            device_id={"dp": target},
            device_id_type=MESH,
        )

    def hop(f, node, kid):
        return remote(
            piece(f, node),
            piece(f, kid),
            send_sem.at[f],
            recv_sem.at[f, slot_of(kid)],
            targets[step_of(node, kid)],
        )

    def across(f, node):
        return remote(piece(f, node), piece(f, node, 1), pair_send.at[f], pair_recv.at[f], sibling)

    pl.semaphore_wait(barrier, len(STEPS) + 1)

    def pass_on(f, node, kids):
        for kid in kids:
            hop(f, node, kid).start()
        across(f, node).start()

    for f, node, kids in ORDER:
        if node == (0, 0) and not (FLOWS[f][1] > PICKED):
            pass_on(f, node, kids)
    for b in range(2):
        for k in range(CHUNKS):
            j = b * CHUNKS + k
            span = pl.ds(k * part, part)
            g, r = loads[j]
            g.wait()
            r.wait()
            acc_out[b, span, :] = rbuf[b, span, :] + gbuf[b, span, :].astype(jnp.float32)
    for b in range(2):
        for i in range(16):
            row = acc_out[b, pl.ds(idx_s[0, b, i], 1), :]
            everyone[0, 0, pl.ds(128 + 16 * b + i, 1), :] = jnp.where(
                i < cnt_s[0, b], row, jnp.float32(0.0)
            )
    for f, node, kids in ORDER:
        if node == (0, 0) and (FLOWS[f][1] > PICKED):
            pass_on(f, node, kids)
    def collect(side, pairs, group):
        way = turn if side == 0 else -turn
        for group, pair in enumerate(pairs, group):
            sums = [None, None]
            for p in range(8):
                rz = 2 * pair + lax.rem(z + p // NY, 2)
                ry = lax.rem(way * (y - p % NY) + NY, NY)
                slot = rz * NY + ry
                for b in range(2):
                    row = everyone[side, slot, pl.ds(126 + b, 1), :]
                    sums[b] = row if sums[b] is None else sums[b] + row
                    block = everyone[side, slot, pl.ds(PICKED + 16 * b, 16), :]
                    high = block.astype(jnp.bfloat16)
                    low = (block - high.astype(jnp.float32)).astype(jnp.bfloat16)
                    k = pl.ds(128 * group + 16 * p, 16)
                    halves[b, k, 0:128] = high
                    halves[b, k, 128:256] = low
            for b in range(2):
                keys[b, :, pl.ds(128 * group, 128)] = sums[b].astype(jnp.int32)

    def sum_tile(t, first_k, keys_n):
        b, first = divmod(t * TILE, nb)
        k = pl.ds(first_k, keys_n)
        row = lax.broadcasted_iota(jnp.int32, (TILE, keys_n), 0) + first
        hit = (row == keys[b, :, k]).astype(jnp.float32).astype(jnp.bfloat16)
        both = jnp.dot(hit, halves[b, k, :], preferred_element_type=jnp.float32)
        tile = both[:, 0:128] + both[:, 128:256]
        if first_k:
            tile = tile + total[b, pl.ds(first, TILE), :]
        total[b, pl.ds(first, TILE), :] = tile

    def settle(f):
        first, last = FLOWS[f][:2]
        span = pl.ds(first, last - first)
        others = everyone.at[0, pl.ds(1, SLOTS - 1), span]
        remote(others, others, send_sem.at[f], pair_recv.at[f], sibling).wait_send()
        pair = remote(everyone.at[0, :, span], everyone.at[1, :, span], pair_send.at[f], pair_recv.at[f], sibling)
        pair.wait_send()
        pair.wait_recv()

    parent = {(f, kid): node for f, node, kids in ORDER for kid in kids}
    later = [entry for entry in ORDER if entry[1] != (0, 0)]
    def add_blocks(side, pairs, group):
        collect(side, pairs, group)
        for t in range(2 * nb // TILE):
            sum_tile(t, 128 * group, 128 * len(pairs))

    sent = max(n for n, entry in enumerate(later) if entry[2])
    here = {entry[1][0] for entry in later[sent + 1 :] if entry[0] == len(FLOWS) - 1}
    pairs = range(NZ // 2)
    whole = [p for p in pairs if not here & {2 * p, 2 * p + 1}]
    for n, (f, node, kids) in enumerate(later):
        hop(f, parent[(f, node)], node).wait_recv()
        pass_on(f, node, kids)
        if n == sent and whole:
            add_blocks(0, whole, 0)
    rest = [p for p in pairs if p not in whole]
    if rest:
        add_blocks(0, rest, len(whole))
    settle(len(FLOWS) - 1)
    add_blocks(1, pairs, len(pairs))
    for f in range(len(FLOWS) - 1):
        settle(f)


def update_kernel(
    sizes, idx_own, cnt, everyone, acc, total, params,
    new_residual, new_momentum, new_params,
    pbuf, nm, mine_v, zero_row, mom_sem, res_sem, row_sem, out_sem,
):
    me = lax.axis_index("dp")
    core = lax.rem(me, 2)
    y = lax.rem(lax.div(me, 2), NY)
    z = lax.div(me, 2 * NY)
    nb = params.shape[1]
    moves = [pltpu.make_async_copy(acc.at[b], new_residual.at[0, b], res_sem.at[b]) for b in range(2)]
    for move in moves:
        move.start()
    zero_row[...] = jnp.zeros_like(zero_row)

    def place_of(o):
        oz, oy, oc = o >> 3, (o >> 1) & 3, o & 1
        turn = 1 - 2 * oc
        slot = ((turn * (z - oz)) & (NZ - 1)) * NY + ((turn * (y - oy)) & (NY - 1))
        return (oc + core) & 1, slot

    part = nb // CHUNKS
    rows = new_momentum.shape[1]
    outs = []
    for b in range(2):

        def place(o, carry):
            start, mine = carry
            side, slot = place_of(o)
            nm[b, pl.ds(start, 64), :] = decay_rate * everyone[side, slot, 63 * b : 63 * b + 64, :]
            return start + sizes[b, o], jnp.where(o == me, start, mine)

        _, first = lax.fori_loop(0, 64, place, (jnp.int32(0), jnp.int32(0)), unroll=8)
        for k in range(CHUNKS):
            span = pl.ds(k * part, part)
            pbuf[b, span, :] = params[b, span, :] - learn_rate * (nm[b, span, :] + total[b, span, :])
            out = pltpu.make_async_copy(pbuf.at[b, span], new_params.at[b, span], out_sem.at[b * CHUNKS + k])
            out.start()
            outs.append(out)
        window = pl.ds(first, rows)
        inside = lax.broadcasted_iota(jnp.int32, (rows, 128), 0) < sizes[b, me]
        mine_v[b] = jnp.where(inside, nm[b, window, :] + total[b, window, :], jnp.float32(0.0))
        out = pltpu.make_async_copy(mine_v.at[b], new_momentum.at[b, :, 0], mom_sem.at[b])
        out.start()
        outs.append(out)

    def clear(b, i):
        return pltpu.make_async_copy(
            zero_row, new_residual.at[0, b, pl.ds(idx_own[0, b, i], 1)], row_sem.at[b, i]
        )

    for b in range(2):
        moves[b].wait()
        for i in range(16):

            @pl.when(i < cnt[0, b])
            def _():
                clear(b, i).start()

    for b in range(2):
        for i in range(16):

            @pl.when(i < cnt[0, b])
            def _():
                clear(b, i).wait()

    for out in outs:
        out.wait()


def on_device(grads, residual, params, momentum, indices, counts, region_sizes):
    nb = grads.shape[2]
    hbm = pl.BlockSpec(memory_space=pltpu.HBM)
    any_space = pl.BlockSpec(memory_space=pl.ANY)
    vmem = pl.BlockSpec(memory_space=pltpu.VMEM)
    smem = pl.BlockSpec(memory_space=pltpu.SMEM)
    dma = pltpu.SemaphoreType.DMA
    everyone, acc, total = pl.pallas_call(
        gather_kernel,
        out_shape=(
            jax.ShapeDtypeStruct((2, SLOTS, ROWS, 128), jnp.float32),
            jax.ShapeDtypeStruct((2, nb, 128), jnp.float32),
            jax.ShapeDtypeStruct((2, PITCH, 128), jnp.float32),
        ),
        in_specs=[hbm] * 5,
        out_specs=(vmem, vmem, vmem),
        scratch_shapes=[
            pltpu.SMEM(indices.shape, jnp.int32),
            pltpu.SMEM(counts.shape, jnp.int32),
            pltpu.VMEM(indices.shape, jnp.int32),
            pltpu.VMEM((2, nb, 128), jnp.bfloat16),
            pltpu.VMEM((2, nb, 128), jnp.float32),
            pltpu.VMEM((2, 1, 1024), jnp.int32),
            pltpu.VMEM((2, 1024, 256), jnp.bfloat16),
            dma((len(FLOWS),)),
            dma((len(FLOWS), SLOTS)),
            dma((len(FLOWS),)),
            dma((len(FLOWS),)),
            dma((2, 2 * CHUNKS)),
            dma((2,)),
            dma((3,)),
        ],
        compiler_params=pltpu.CompilerParams(
            collective_id=0, has_side_effects=True, vmem_limit_bytes=32 << 20
        ),
        name="gather",
    )(*(pltpu.with_memory_space_constraint(a, pltpu.HBM) for a in (indices, counts, grads, residual, jnp.swapaxes(momentum, 1, 2))))
    rows = momentum.shape[2]
    new_residual, new_momentum, new_params = pl.pallas_call(
        update_kernel,
        out_shape=(
            jax.ShapeDtypeStruct((1, 2, nb, 128), jnp.float32),
            jax.ShapeDtypeStruct((2, rows, 1, 128), jnp.float32),
            jax.ShapeDtypeStruct(params.shape, jnp.float32),
        ),
        in_specs=[smem, smem, smem, vmem, vmem, vmem, vmem],
        out_specs=(any_space, any_space, any_space),
        scratch_shapes=[
            pltpu.VMEM((2, nb, 128), jnp.float32),
            pltpu.VMEM((2, PITCH, 128), jnp.float32),
            pltpu.VMEM((2, rows, 128), jnp.float32),
            pltpu.VMEM((1, 128), jnp.float32),
            dma((2,)),
            dma((2,)),
            dma((2, 16)),
            dma((2 * CHUNKS,)),
        ],
        compiler_params=pltpu.CompilerParams(vmem_limit_bytes=32 << 20),
        name="update",
    )(region_sizes, indices, counts, everyone, acc, total, params)
    return new_residual, jnp.swapaxes(new_momentum, 1, 2), new_params


def solution(mesh):
    placed = (
        P("dp", "grp", None, None),
        P("dp", "grp", None, None),
        P("grp", None, None),
        P("grp", "dp", None, None),
        P("dp", "grp", None),
        P("dp", "grp"),
        P("grp", None),
    )
    return jax.shard_map(
        on_device,
        mesh=mesh,
        in_specs=placed,
        out_specs=(P("dp", "grp", None, None), P("grp", "dp", None, None), P("grp", None, None)),
        check_vma=False,
    )
```

```python
import functools
import heapq

import jax
import jax.numpy as jnp
from jax import lax
from jax.experimental import pallas as pl
from jax.experimental.pallas import tpu as pltpu
from jax.sharding import PartitionSpec as P

decay_rate = 0.9
learn_rate = 0.1

NZ, NY = 8, 4
SLOTS = NZ * NY
ROWS = 160
MESH = pl.DeviceIdType.MESH
CHUNKS = 4
TILE = 512
PICKED = 128
PITCH = 2048 + 64


FLOWS = (
    (0, 80, (0, 0, 22, 0, 0, 4, 5, 3, 4, 13, 6, 7, 8, 12, 15, 12, 12, 16, 22, 16, 23, 20, 23, 3, 20, 24, 22, 31, 0, 28, 31, 28)),
    (80, 160, (0, 0, 0, 2, 5, 6, 2, 6, 0, 8, 8, 10, 8, 12, 10, 12, 24, 16, 26, 18, 12, 20, 26, 20, 0, 24, 2, 31, 0, 28, 31, 28)),
)


def tree_of(flow):
    children = {(rz, ry): [] for rz in range(NZ) for ry in range(NY)}
    for slot, parent in enumerate(flow[2]):
        if slot:
            children[divmod(parent, NY)].append(divmod(slot, NY))
    return children


TREES = tuple(tree_of(flow) for flow in FLOWS)


def step_of(node, kid):
    dz, dy = (kid[0] - node[0]) % NZ, (kid[1] - node[1]) % NY
    return (dz if 2 * dz <= NZ else dz - NZ), (dy if 2 * dy <= NY else dy - NY)


STEPS = tuple(sorted({step_of(n, k) for t in TREES for n, kids in t.items() for k in kids}))
LATENCY, PER_HOP, PICKS = 2.0, 0.65, 1.5


def schedule():
    def height(f, node):
        return 1 + max((height(f, c) for c in TREES[f][node]), default=0)

    heap = [(PICKS if (FLOWS[f][1] > PICKED) else 0.0, f, (0, 0)) for f in range(len(FLOWS))]
    free = {"z": 0.0, "y": 0.0}
    now, order = 0.0, []
    while heap:
        at, f, node = heapq.heappop(heap)
        now = max(now, at) + 0.02
        kids = sorted(TREES[f][node], key=lambda c: -height(f, c))
        order.append((f, node, kids))
        for kid in kids:
            now += 0.02
            dz, dy = step_of(node, kid)
            axis, hops = ("z", abs(dz)) if dz else ("y", abs(dy))
            free[axis] = max(free[axis], now) + hops * (FLOWS[f][1] - FLOWS[f][0]) * 512 / 102e3
            heapq.heappush(heap, (free[axis] + LATENCY + hops * PER_HOP, f, kid))
    return order


ORDER = schedule()


def slot_of(node):
    return node[0] * NY + node[1]


def gather_kernel(
    idx, cnt, grads, residual, momentum,
    everyone, acc_out, total,
    idx_s, cnt_s, idx_v, gbuf, rbuf, keys, halves,
    send_sem, recv_sem, pair_send, pair_recv, in_sem, mom_sem, small_sem,
):
    me = lax.axis_index("dp")
    core = lax.rem(me, 2)
    y = lax.rem(lax.div(me, 2), NY)
    z = lax.div(me, 2 * NY)
    turn = 1 - 2 * core

    def at(dz, dy):
        return (lax.rem(z + turn * dz + NZ, NZ) * NY + lax.rem(y + turn * dy + NY, NY)) * 2 + core

    sibling = me + turn
    targets = {step: at(*step) for step in STEPS}

    barrier = pltpu.get_barrier_semaphore()
    for t in [at(-dz, -dy) for dz, dy in STEPS] + [sibling]:
        pl.semaphore_signal(barrier, inc=1, device_id={"dp": t}, device_id_type=MESH)

    nb = residual.shape[2]
    part = nb // CHUNKS
    small = [
        pltpu.make_async_copy(idx, idx_v, small_sem.at[0]),
        pltpu.make_async_copy(idx, idx_s, small_sem.at[1]),
        pltpu.make_async_copy(cnt, cnt_s, small_sem.at[2]),
    ]
    for b in range(2):
        small.append(
            pltpu.make_async_copy(
                momentum.at[b, :, 0], everyone.at[0, 0, pl.ds(63 * b, 63)], mom_sem.at[b]
            )
        )
    for copy in small:
        copy.start()
    loads = []
    for b in range(2):
        for k in range(CHUNKS):
            span = pl.ds(k * part, part)
            j = b * CHUNKS + k
            g = pltpu.make_async_copy(grads.at[0, b, span], gbuf.at[b, span], in_sem.at[0, j])
            r = pltpu.make_async_copy(residual.at[0, b, span], rbuf.at[b, span], in_sem.at[1, j])
            g.start()
            r.start()
            loads.append((g, r))
    for copy in small:
        copy.wait()
    lists = idx_v[0].astype(jnp.float32)
    lane = lax.broadcasted_iota(jnp.int32, (1, 128), 1)
    own = lax.div(lane, 16) == lax.rem(z, 2) * NY + y
    for b in range(2):
        at_row = pl.ds(126 + b, 1)
        for q in range(8):
            everyone[0, 0, at_row, 16 * q : 16 * q + 16] = lists[b : b + 1]
        everyone[0, 0, at_row, :] = jnp.where(own, everyone[0, 0, at_row, :], jnp.float32(0.0))

    def piece(f, node, side=0):
        first, last = FLOWS[f][:2]
        return everyone.at[side, slot_of(node), pl.ds(first, last - first)]

    def remote(src, dst, sent, received, target):
        return pltpu.make_async_remote_copy(
            src_ref=src,
            dst_ref=dst,
            send_sem=sent,
            recv_sem=received,
            device_id={"dp": target},
            device_id_type=MESH,
        )

    def hop(f, node, kid):
        return remote(
            piece(f, node),
            piece(f, kid),
            send_sem.at[f],
            recv_sem.at[f, slot_of(kid)],
            targets[step_of(node, kid)],
        )

    def across(f, node):
        arrived = f + node[0] // 2 if f == len(FLOWS) - 1 else f
        return remote(piece(f, node), piece(f, node, 1), pair_send.at[f], pair_recv.at[arrived], sibling)

    pl.semaphore_wait(barrier, len(STEPS) + 1)

    def pass_on(f, node, kids):
        for kid in kids:
            hop(f, node, kid).start()
        across(f, node).start()

    for f, node, kids in ORDER:
        if node == (0, 0) and not (FLOWS[f][1] > PICKED):
            pass_on(f, node, kids)
    for b in range(2):
        for k in range(CHUNKS):
            j = b * CHUNKS + k
            span = pl.ds(k * part, part)
            g, r = loads[j]
            g.wait()
            r.wait()
            acc_out[b, span, :] = rbuf[b, span, :] + gbuf[b, span, :].astype(jnp.float32)
    for b in range(2):
        for i in range(16):
            row = acc_out[b, pl.ds(idx_s[0, b, i], 1), :]
            everyone[0, 0, pl.ds(128 + 16 * b + i, 1), :] = jnp.where(
                i < cnt_s[0, b], row, jnp.float32(0.0)
            )
    for f, node, kids in ORDER:
        if node == (0, 0) and (FLOWS[f][1] > PICKED):
            pass_on(f, node, kids)
    def collect(side, pairs, group):
        way = turn if side == 0 else -turn
        for group, pair in enumerate(pairs, group):
            sums = [None, None]
            for p in range(8):
                rz = 2 * pair + lax.rem(z + p // NY, 2)
                ry = lax.rem(way * (y - p % NY) + NY, NY)
                slot = rz * NY + ry
                for b in range(2):
                    row = everyone[side, slot, pl.ds(126 + b, 1), :]
                    sums[b] = row if sums[b] is None else sums[b] + row
                    block = everyone[side, slot, pl.ds(PICKED + 16 * b, 16), :]
                    high = block.astype(jnp.bfloat16)
                    low = (block - high.astype(jnp.float32)).astype(jnp.bfloat16)
                    k = pl.ds(128 * group + 16 * p, 16)
                    halves[b, k, 0:128] = high
                    halves[b, k, 128:256] = low
            for b in range(2):
                keys[b, :, pl.ds(128 * group, 128)] = sums[b].astype(jnp.int32)

    def sum_tile(t, first_k, keys_n):
        b, first = divmod(t * TILE, nb)
        k = pl.ds(first_k, keys_n)
        row = lax.broadcasted_iota(jnp.int32, (TILE, keys_n), 0) + first
        hit = (row == keys[b, :, k]).astype(jnp.float32).astype(jnp.bfloat16)
        both = jnp.dot(hit, halves[b, k, :], preferred_element_type=jnp.float32)
        tile = both[:, 0:128] + both[:, 128:256]
        if first_k:
            tile = tile + total[b, pl.ds(first, TILE), :]
        total[b, pl.ds(first, TILE), :] = tile

    def settle(f):
        first, last = FLOWS[f][:2]
        span = pl.ds(first, last - first)
        others = everyone.at[0, pl.ds(1, SLOTS - 1), span]
        remote(others, others, send_sem.at[f], pair_recv.at[f], sibling).wait_send()
        pair = remote(everyone.at[0, :, span], everyone.at[1, :, span], pair_send.at[f], pair_recv.at[f], sibling)
        pair.wait_send()
        if f < len(FLOWS) - 1:
            pair.wait_recv()

    parent = {(f, kid): node for f, node, kids in ORDER for kid in kids}
    later = [entry for entry in ORDER if entry[1] != (0, 0)]
    def add_blocks(group, *parts):
        count = 0
        for side, some in parts:
            collect(side, some, group + count)
            count += len(some)
        for t in range(2 * nb // TILE):
            sum_tile(t, 128 * group, 128 * count)

    def arrive(some):
        first, last = FLOWS[-1][:2]
        span = pl.ds(first, last - first)
        for p in some:
            slots = pl.ds(2 * NY * p, 2 * NY)
            remote(
                everyone.at[0, slots, span],
                everyone.at[1, slots, span],
                pair_send.at[len(FLOWS) - 1],
                pair_recv.at[len(FLOWS) - 1 + p],
                sibling,
            ).wait_recv()

    sent = max(n for n, entry in enumerate(later) if entry[2])
    here = {entry[1][0] for entry in later[sent + 1 :] if entry[0] == len(FLOWS) - 1}
    pairs = range(NZ // 2)
    whole = [p for p in pairs if not here & {2 * p, 2 * p + 1}]
    for n, (f, node, kids) in enumerate(later):
        hop(f, parent[(f, node)], node).wait_recv()
        pass_on(f, node, kids)
        if n == sent and whole:
            arrive(whole)
            add_blocks(0, (0, whole), (1, whole))
    rest = [p for p in pairs if p not in whole]
    if rest:
        add_blocks(2 * len(whole), (0, rest))
        arrive(rest)
        add_blocks(2 * len(whole) + len(rest), (1, rest))
    for f in range(len(FLOWS)):
        settle(f)


def update_kernel(
    sizes, idx_own, cnt, everyone, acc, total, params,
    new_residual, new_momentum, new_params,
    pbuf, nm, mine_v, zero_row, mom_sem, res_sem, row_sem, out_sem,
):
    me = lax.axis_index("dp")
    core = lax.rem(me, 2)
    y = lax.rem(lax.div(me, 2), NY)
    z = lax.div(me, 2 * NY)
    nb = params.shape[1]
    moves = [pltpu.make_async_copy(acc.at[b], new_residual.at[0, b], res_sem.at[b]) for b in range(2)]
    for move in moves:
        move.start()
    zero_row[...] = jnp.zeros_like(zero_row)

    def place_of(o):
        oz, oy, oc = o >> 3, (o >> 1) & 3, o & 1
        turn = 1 - 2 * oc
        slot = ((turn * (z - oz)) & (NZ - 1)) * NY + ((turn * (y - oy)) & (NY - 1))
        return (oc + core) & 1, slot

    part = nb // CHUNKS
    rows = new_momentum.shape[1]
    outs = []
    for b in range(2):

        def place(o, carry):
            start, mine = carry
            side, slot = place_of(o)
            nm[b, pl.ds(start, 64), :] = decay_rate * everyone[side, slot, 63 * b : 63 * b + 64, :]
            return start + sizes[b, o], jnp.where(o == me, start, mine)

        _, first = lax.fori_loop(0, 64, place, (jnp.int32(0), jnp.int32(0)), unroll=8)
        for k in range(CHUNKS):
            span = pl.ds(k * part, part)
            pbuf[b, span, :] = params[b, span, :] - learn_rate * (nm[b, span, :] + total[b, span, :])
            out = pltpu.make_async_copy(pbuf.at[b, span], new_params.at[b, span], out_sem.at[b * CHUNKS + k])
            out.start()
            outs.append(out)
        window = pl.ds(first, rows)
        inside = lax.broadcasted_iota(jnp.int32, (rows, 128), 0) < sizes[b, me]
        mine_v[b] = jnp.where(inside, nm[b, window, :] + total[b, window, :], jnp.float32(0.0))
        out = pltpu.make_async_copy(mine_v.at[b], new_momentum.at[b, :, 0], mom_sem.at[b])
        out.start()
        outs.append(out)

    def clear(b, i):
        return pltpu.make_async_copy(
            zero_row, new_residual.at[0, b, pl.ds(idx_own[0, b, i], 1)], row_sem.at[b, i]
        )

    for b in range(2):
        moves[b].wait()
        for i in range(16):

            @pl.when(i < cnt[0, b])
            def _():
                clear(b, i).start()

    for b in range(2):
        for i in range(16):

            @pl.when(i < cnt[0, b])
            def _():
                clear(b, i).wait()

    for out in outs:
        out.wait()


def on_device(grads, residual, params, momentum, indices, counts, region_sizes):
    nb = grads.shape[2]
    hbm = pl.BlockSpec(memory_space=pltpu.HBM)
    any_space = pl.BlockSpec(memory_space=pl.ANY)
    vmem = pl.BlockSpec(memory_space=pltpu.VMEM)
    smem = pl.BlockSpec(memory_space=pltpu.SMEM)
    dma = pltpu.SemaphoreType.DMA
    everyone, acc, total = pl.pallas_call(
        gather_kernel,
        out_shape=(
            jax.ShapeDtypeStruct((2, SLOTS, ROWS, 128), jnp.float32),
            jax.ShapeDtypeStruct((2, nb, 128), jnp.float32),
            jax.ShapeDtypeStruct((2, PITCH, 128), jnp.float32),
        ),
        in_specs=[hbm] * 5,
        out_specs=(vmem, vmem, vmem),
        scratch_shapes=[
            pltpu.SMEM(indices.shape, jnp.int32),
            pltpu.SMEM(counts.shape, jnp.int32),
            pltpu.VMEM(indices.shape, jnp.int32),
            pltpu.VMEM((2, nb, 128), jnp.bfloat16),
            pltpu.VMEM((2, nb, 128), jnp.float32),
            pltpu.VMEM((2, 1, 1024), jnp.int32),
            pltpu.VMEM((2, 1024, 256), jnp.bfloat16),
            dma((len(FLOWS),)),
            dma((len(FLOWS), SLOTS)),
            dma((len(FLOWS),)),
            dma((len(FLOWS) + NZ // 2 - 1,)),
            dma((2, 2 * CHUNKS)),
            dma((2,)),
            dma((3,)),
        ],
        compiler_params=pltpu.CompilerParams(
            collective_id=0, has_side_effects=True, vmem_limit_bytes=32 << 20
        ),
        name="gather",
    )(*(pltpu.with_memory_space_constraint(a, pltpu.HBM) for a in (indices, counts, grads, residual, jnp.swapaxes(momentum, 1, 2))))
    rows = momentum.shape[2]
    new_residual, new_momentum, new_params = pl.pallas_call(
        update_kernel,
        out_shape=(
            jax.ShapeDtypeStruct((1, 2, nb, 128), jnp.float32),
            jax.ShapeDtypeStruct((2, rows, 1, 128), jnp.float32),
            jax.ShapeDtypeStruct(params.shape, jnp.float32),
        ),
        in_specs=[smem, smem, smem, vmem, vmem, vmem, vmem],
        out_specs=(any_space, any_space, any_space),
        scratch_shapes=[
            pltpu.VMEM((2, nb, 128), jnp.float32),
            pltpu.VMEM((2, PITCH, 128), jnp.float32),
            pltpu.VMEM((2, rows, 128), jnp.float32),
            pltpu.VMEM((1, 128), jnp.float32),
            dma((2,)),
            dma((2,)),
            dma((2, 16)),
            dma((2 * CHUNKS,)),
        ],
        compiler_params=pltpu.CompilerParams(vmem_limit_bytes=32 << 20),
        name="update",
    )(region_sizes, indices, counts, everyone, acc, total, params)
    return new_residual, jnp.swapaxes(new_momentum, 1, 2), new_params


def solution(mesh):
    placed = (
        P("dp", "grp", None, None),
        P("dp", "grp", None, None),
        P("grp", None, None),
        P("grp", "dp", None, None),
        P("dp", "grp", None),
        P("dp", "grp"),
        P("grp", None),
    )
    return jax.shard_map(
        on_device,
        mesh=mesh,
        in_specs=placed,
        out_specs=(P("dp", "grp", None, None), P("grp", "dp", None, None), P("grp", None, None)),
        check_vma=False,
    )
```
